32 devices in a mesh: feat: 8 (over y, x, core), layer: 4 (over z).
Axes of the slice: x: 2, y: 2, z: 4, core: 2. Of those that a mesh axis runs over, the one named last changes fastest.
Arguments:
- residual_in: bfloat16 [4, 24, 2304], P('layer', 'feat'), as said below
- enc_weight: bfloat16 [4, 2304, 8192], P('layer', None, 'feat'), as said below
- thresholds: int32 [4, 8192], P('layer', 'feat'), may hold values from -2016 to 7341, as said below
- dec_weight: bfloat16 [4, 4, 8192, 2304], P(None, 'layer', 'feat'), may hold values from -0.03125 to 0.03125
- target: bfloat16 [4, 24, 2304], P('layer', 'feat')
Outputs:
- loss_value: float32 [], replicated
- reconstruction: bfloat16 [4, 24, 2304], P('layer', 'feat')
- dec_grad: bfloat16 [4, 4, 8192, 2304], P(None, 'layer', 'feat')
- enc_grad: bfloat16 [4, 2304, 8192], P('layer', None, 'feat')
The draws below stay inside these ranges and needn't reach their ends.
Inputs may be any that keep to these rules, and one draw needn't show every extreme that they name: `residual_in`: every entry is a multiple of 1/8. `enc_weight`: every entry is a multiple of 1/256. `thresholds`: whole numbers.
All inputs are finite; a program needn't handle non-finite values.
Results may differ from the reference program's by a relative error of at most 0.007.
Values may be sent and summed in bfloat16 or wider, within the bound.
No kernel may reach another device: no remote copies, remote signals or barrier semaphores. Data moves between devices by JAX's collectives and lax.ppermute only.
A program may use at most 128 MiB of HBM per device.

```python
import jax
import jax.numpy as jnp

D = 2304
FEAT = 8192
NSRC = 4
NTGT = 4
TOKENS = 24


def column_factor():
    return 1 + 3 * jnp.arange(FEAT, dtype=jnp.int32) // FEAT


def draw_residual_in(key, part):
    levels = jax.random.randint(key, (NSRC, TOKENS, D), -16, 17)
    return (levels.astype(jnp.float32) / 8.0).astype(jnp.bfloat16)


def draw_enc_weight(key, part):
    levels = jax.random.randint(key, (NSRC, D, FEAT), -8, 9)
    scaled = levels * column_factor()[None, None, :]
    return (scaled.astype(jnp.float32) / 256.0).astype(jnp.bfloat16)


def draw_thresholds(key, part):
    spread = min(D // 8, 48)
    levels = jax.random.randint(key, (NSRC, FEAT), -14 * spread, 51 * spread)
    levels = levels.at[0, FEAT - 1].set(51 * spread - 1)
    levels = levels.at[0, FEAT - 2].set(-14 * spread)
    return (levels * column_factor()[None, :]).astype(jnp.int32)


def draw_target(key, part):
    row_index = jnp.arange(TOKENS, dtype=jnp.float32)
    row_scale = 1.0 + 3.0 * row_index / TOKENS
    values = jax.random.normal(key, (NTGT, TOKENS, D))
    return (values * row_scale[None, :, None]).astype(jnp.bfloat16)


def level_of(key, dims, cuts, low, high):
    factor_of = 1.0
    for dim, shards_of in cuts:
        heights = jax.random.uniform(jax.random.fold_in(jax.random.fold_in(key, 6), dim), (shards_of,), jnp.float32, low / len(cuts), high / len(cuts))
        factor_of = factor_of * jnp.repeat(jnp.exp(heights), dims[dim] // shards_of).reshape((-1,) + (1,) * (len(dims) - 1 - dim))
    return factor_of


def scatter_about(own_key, shape, scale, limit, shards=(), kind=jnp.bfloat16):
    array = jax.random.normal(own_key, shape, jnp.float32) * scale
    if len(shards) > 0:
        array = level_of(own_key, shape, shards, -0.22, 0.18) * array
    return jnp.clip(array, min=-limit, max=limit).astype(kind)


def setup_inputs(seed: int = 0) -> dict:
    streams_of = jax.random.split(jax.random.key(seed), 6)
    return {
        "residual_in": draw_residual_in(jax.random.fold_in(streams_of[5], 71), 0),
        "enc_weight": draw_enc_weight(jax.random.fold_in(streams_of[5], 71), 0),
        "thresholds": draw_thresholds(jax.random.fold_in(streams_of[5], 71), 0),
        "dec_weight": scatter_about(streams_of[3], (NSRC, NTGT, FEAT, D), (NSRC * FEAT) ** -0.5, 0.03125, ((1, 4), (2, 8))),
        "target": draw_target(jax.random.fold_in(streams_of[5], 71), 0),
    }


ERROR_SCALE = 32.0
PENALTY_WEIGHT = 4.0


def reference(residual_in, enc_weight, thresholds, dec_weight, target):
    jump_level = (thresholds.astype(jnp.float32) + 0.5) / 2048.0
    preactivation = jnp.stack([jnp.dot(residual_in[source], enc_weight[source], preferred_element_type=jnp.float32) for source in range(NSRC)])
    active_mask = preactivation > jump_level[:, None, :]
    feature_activations = jnp.where(active_mask, preactivation, 0.0).astype(jnp.bfloat16)
    magnitude = jnp.mean(jnp.abs(feature_activations.astype(jnp.float32)), axis=1)
    penalty = jnp.sum(magnitude * magnitude)
    outputs = []
    for layer_out in range(NTGT):
        summed = jnp.dot(feature_activations[0], dec_weight[0, layer_out], preferred_element_type=jnp.float32)
        for source in range(1, NSRC):
            summed = summed + jnp.dot(feature_activations[source], dec_weight[source, layer_out], preferred_element_type=jnp.float32)
        outputs.append(summed)
    recon = jnp.stack(outputs)
    error_rows = recon - target.astype(jnp.float32)
    squares = jnp.sum(error_rows * error_rows)
    loss_value = (squares + 2.0 * ERROR_SCALE * PENALTY_WEIGHT * penalty) / (NTGT * TOKENS * D)
    grad = (error_rows / ERROR_SCALE).astype(jnp.bfloat16)
    dec_grad = jnp.stack([jnp.stack([jnp.dot(feature_activations[source].T, grad[layer_out], preferred_element_type=jnp.float32).astype(jnp.bfloat16) for layer_out in range(NTGT)]) for source in range(NSRC)])
    act_list = []
    for source in range(NSRC):
        summed = jnp.dot(grad[0], dec_weight[source, 0].T, preferred_element_type=jnp.float32)
        for layer_out in range(1, NTGT):
            summed = summed + jnp.dot(grad[layer_out], dec_weight[source, layer_out].T, preferred_element_type=jnp.float32)
        act_list.append(summed)
    activation_gradient = jnp.stack(act_list)
    sparsity_gradient = 2.0 * PENALTY_WEIGHT * magnitude[:, None, :] * jnp.sign(feature_activations.astype(jnp.float32)) / TOKENS
    preactivation_gradient = jnp.where(active_mask, activation_gradient + sparsity_gradient, 0.0).astype(jnp.bfloat16)
    enc_grad = jnp.stack([jnp.dot(residual_in[source].T, preactivation_gradient[source], preferred_element_type=jnp.float32).astype(jnp.bfloat16) for source in range(NSRC)])
    return (loss_value, recon.astype(jnp.bfloat16), dec_grad, enc_grad)
```

```python
import functools

import jax
import jax.numpy as jnp
from jax import lax
from jax.experimental import pallas as pl
from jax.experimental.pallas import tpu as pltpu
from jax.sharding import PartitionSpec as P

ERROR_SCALE = 32.0
PENALTY_WEIGHT = 4.0
F32 = jnp.float32
BF16 = jnp.bfloat16
LANES = 128
MIB = 1 << 20
WHOLE = pl.BlockSpec(memory_space=pltpu.VMEM)
ANY = pl.BlockSpec(memory_space=pl.ANY)
NT = (((1,), (1,)), ((), ()))
TN = (((0,), (0,)), ((), ()))


def in_vmem(x):
    return pltpu.with_memory_space_constraint(x, pltpu.VMEM)


def shape(dims, dtype):
    return jax.ShapeDtypeStruct(dims, dtype)


def call(body, outs, args, name, scratch=(), limit=16, in_specs=None, out_specs=None, flops=0, bytes_accessed=0):
    return pl.pallas_call(
        body,
        out_shape=outs,
        in_specs=in_specs or [WHOLE] * len(args),
        out_specs=out_specs or [WHOLE] * len(outs),
        scratch_shapes=list(scratch),
        compiler_params=pltpu.CompilerParams(vmem_limit_bytes=limit * MIB),
        cost_estimate=pl.CostEstimate(flops=flops, bytes_accessed=bytes_accessed, transcendentals=0),
        name=name,
    )(*args)


def swap(x, axis, bits):
    size = lax.axis_size(axis)
    return lax.ppermute(x, axis, [(i, i ^ bits) for i in range(size)])


def split3(value):
    high = value.astype(BF16)
    rest = value - high.astype(F32)
    middle = rest.astype(BF16)
    low = (rest - middle.astype(F32)).astype(BF16)
    return high, middle, low


def spread3(value, dims):
    high, middle, low = (part.astype(F32) for part in split3(value))
    lane = lax.broadcasted_iota(jnp.int32, dims, 1)
    block = jnp.where(lane == 0, high, jnp.where(lane == 1, middle, jnp.where(lane == 2, low, 0.0)))
    return block.astype(BF16)


def encode(x_ref, enc_ref, thr_ref, acts_ref, gate_ref, sparse_ref, pen_ref):
    tokens = x_ref.shape[0]
    cutoff = (thr_ref[...].astype(F32) + 0.5) / 2048.0
    preact = jnp.dot(x_ref[...], enc_ref[...], preferred_element_type=F32)
    firing = preact > cutoff
    acts = jnp.where(firing, preact, 0.0).astype(BF16)
    acts_ref[...] = acts
    wide = acts.astype(F32)
    magnitude = jnp.sum(jnp.abs(wide), axis=0, keepdims=True) / tokens
    sign = jnp.where(wide > 0, 1.0, jnp.where(wide < 0, -1.0, 0.0))
    gate_ref[...] = firing.astype(F32)
    sparse_ref[...] = 2.0 * PENALTY_WEIGHT * magnitude * sign / tokens
    pen = jnp.sum(magnitude * magnitude, axis=1, keepdims=True)
    pen_ref[...] = jnp.broadcast_to(pen, pen_ref.shape)


def recon_own(acts_ref, dec_hbm, dec_ref, total_ref, sems):
    sources = dec_hbm.shape[0]
    me = lax.axis_index("layer")
    copies = []
    for k in range(sources):
        copies.append(pltpu.make_async_copy(dec_hbm.at[me ^ k], dec_ref.at[me ^ k], sems.at[k]))
        copies[-1].start()
    copies[0].wait()
    total_ref[...] = jnp.dot(acts_ref[...], dec_ref[me], preferred_element_type=F32)
    for k in range(1, sources):
        copies[k].wait()


def recon_rest(*refs):
    total_ref, pen_ref, dec_ref, *acts = refs[:-2]
    keep_ref, send_ref = refs[-2:]
    me = lax.axis_index("layer")
    half = dec_ref.shape[2] // 2
    total = total_ref[...]
    for k, acts_ref in enumerate(acts, 1):
        total = total + jnp.dot(acts_ref[...], dec_ref[me ^ k], preferred_element_type=F32)
    first, second = total[:, :half], total[:, half:]
    low = lax.axis_index("feat") % 2 == 0
    pen = jnp.broadcast_to(pen_ref[0:1, :], (total.shape[0], LANES))
    keep_ref[:, :half] = jnp.where(low, first, second)
    send_ref[:, :half] = jnp.where(low, second, first)
    keep_ref[:, half:] = pen
    send_ref[:, half:] = pen


def pair_sum(keep_ref, got_ref, msg_ref):
    half = keep_ref.shape[1] - LANES
    msg_ref[:, :half] = (keep_ref[:, :half] + got_ref[:, :half]).astype(BF16)
    pen = keep_ref[0:1, half : half + 1] + got_ref[0:1, half : half + 1]
    msg_ref[:, half:] = spread3(pen, (keep_ref.shape[0], LANES))


def sum_messages(refs):
    terms = [ref[...].astype(F32) for ref in refs]
    while len(terms) > 1:
        terms = [terms[i] + terms[i + 1] for i in range(0, len(terms), 2)]
    return terms[0]


def group_sum(*refs):
    half = refs[0].shape[1] - LANES
    total = sum_messages(refs[:-1])
    refs[-1][:, :half] = total[:, :half].astype(BF16)
    pen = jnp.sum(total[0:1, half:], axis=1, keepdims=True)
    refs[-1][:, half:] = spread3(pen, (total.shape[0], LANES))


def pick_rows(device, rows, tokens):
    row = lax.broadcasted_iota(jnp.int32, (8, tokens), 0)
    column = lax.broadcasted_iota(jnp.int32, (8, tokens), 1)
    return jnp.where((column == device * rows + row) & (row < rows), 1.0, 0.0).astype(BF16)


def error_half(rows, target_ref, *refs):
    *msgs, out_ref, own_ref, pen_ref = refs
    tokens, half = target_ref.shape[0], target_ref.shape[1] // 2
    me = lax.axis_index("feat")
    total = sum_messages(msgs)
    recon = total[:, :half]
    target = jnp.where(me % 2 == 0, target_ref[:, :half], target_ref[:, half:]).astype(F32)
    error = recon - target
    squares = jnp.sum(jnp.sum(error * error, axis=1, keepdims=True), axis=0, keepdims=True)
    narrow = recon.astype(BF16)
    own_ref[...] = jnp.dot(pick_rows(me, rows, tokens), narrow, preferred_element_type=F32)
    theirs = jnp.dot(pick_rows(me ^ 1, rows, tokens), narrow, preferred_element_type=F32)
    row = lax.broadcasted_iota(jnp.int32, (8, half), 0)
    parts = spread3(squares, (8, LANES)).astype(F32)
    parts = jnp.concatenate([parts, jnp.zeros((8, half - LANES), F32)], axis=1)
    out_ref[:tokens, :] = (error / ERROR_SCALE).astype(BF16)
    out_ref[tokens:, :] = jnp.where(row < rows, theirs, jnp.where(row == rows, parts, 0.0)).astype(BF16)
    pen = jnp.sum(total[0:1, half:], axis=1, keepdims=True)
    pen_ref[...] = jnp.broadcast_to(pen, pen_ref.shape)


def act_grads(rows, mine_ref, got_ref, own_ref, pen_ref, dec_ref, *outs):
    recon_ref, grad_ref, score_ref, part_ref, *msgs = outs
    tokens, half = grad_ref.shape[0], grad_ref.shape[1] // 2
    low = lax.axis_index("feat") % 2 == 0
    me = lax.axis_index("layer")
    first = jnp.where(low, mine_ref[:tokens, :], got_ref[:tokens, :])
    second = jnp.where(low, got_ref[:tokens, :], mine_ref[:tokens, :])
    grad_ref[:, :half] = first
    grad_ref[:, half:] = second
    extra = got_ref[tokens:, :].astype(F32)
    own = own_ref[...]
    recon_ref[:, :half] = jnp.where(low, own, extra)[:rows].astype(BF16)
    recon_ref[:, half:] = jnp.where(low, extra, own)[:rows].astype(BF16)
    mine_extra = mine_ref[tokens:, :].astype(F32)
    squares = jnp.sum(mine_extra[rows : rows + 1, :LANES], axis=1, keepdims=True)
    squares = squares + jnp.sum(extra[rows : rows + 1, :LANES], axis=1, keepdims=True)
    score = squares + 2.0 * ERROR_SCALE * PENALTY_WEIGHT * pen_ref[0:1, 0:1]
    score_ref[...] = jnp.broadcast_to(score, score_ref.shape)
    grad = grad_ref[...]
    width = dec_ref.shape[1]
    for k in range(len(msgs), -1, -1):
        part = lax.dot_general(grad, dec_ref[me ^ k], NT, preferred_element_type=F32)
        if k:
            msgs[k - 1][:, :width] = part.astype(BF16)
            msgs[k - 1][:, width:] = spread3(score, (tokens, LANES))
        else:
            part_ref[...] = part


def decoder_grads(steps, grad_ref, *refs):
    *acts, out_hbm, buf, sems = refs
    me = lax.axis_index("layer")
    features = acts[0].shape[1]
    block = features // steps
    grad = grad_ref[...]
    copies = []
    for k, acts_ref in enumerate(acts):
        for i in range(steps):
            slot = len(copies) % 2
            if len(copies) >= 2:
                copies[-2].wait()
            span = pl.ds(i * block, block)
            value = lax.dot_general(acts_ref[:, span], grad, TN, preferred_element_type=F32)
            buf[slot] = value.astype(BF16)
            copies.append(pltpu.make_async_copy(buf.at[slot], out_hbm.at[me ^ k, span], sems.at[slot]))
            copies[-1].start()
    for copy in copies[-2:]:
        copy.wait()


def encoder_grad(count, x_ref, part_ref, gate_ref, sparse_ref, score_ref, *refs):
    *msgs, out_ref, loss_ref, pre_ref = refs
    width = part_ref.shape[1]

    @pl.when(pl.program_id(0) == 0)
    def _():
        total = part_ref[...]
        for msg in msgs:
            total = total + msg[:, :width].astype(F32)
        pre = jnp.where(gate_ref[...] > 0, total + sparse_ref[...], 0.0)
        pre_ref[...] = pre.astype(BF16)
        scores = [score_ref[0:1, 0:1]]
        for msg in msgs:
            scores.append(jnp.sum(msg[0:1, width:].astype(F32), axis=1, keepdims=True))
        while len(scores) > 1:
            scores = [scores[i] + scores[i + 1] for i in range(0, len(scores), 2)]
        loss_ref[...] = scores[0] / count

    out_ref[...] = lax.dot_general(x_ref[...], pre_ref[...], TN, preferred_element_type=F32).astype(BF16)


def body(residual_in, enc_weight, thresholds, dec_weight, target):
    layers, feats = lax.axis_size("layer"), lax.axis_size("feat")
    rows, width = residual_in.shape[1:]
    features = enc_weight.shape[2]
    tokens, half = rows * feats, width // 2
    sources = dec_weight.shape[0]
    decoder = dec_weight[:, 0]

    inputs = lax.all_gather(jnp.concatenate([residual_in, target]), "feat", axis=1, tiled=True)
    x, targets = inputs[0], inputs[1]

    acts, gate, sparse, pen = call(
        encode,
        [shape((tokens, features), BF16), shape((tokens, features), F32), shape((tokens, features), F32), shape((8, LANES), F32)],
        (x, in_vmem(enc_weight[0]), thresholds),
        "encode",
        flops=2 * tokens * width * features,
        bytes_accessed=2 * width * features,
    )
    others = [swap(acts, "layer", k) for k in range(1, layers)]
    dec, total = call(
        recon_own,
        [pltpu.VMEM((sources, features, width), BF16), shape((tokens, width), F32)],
        (acts, decoder),
        "recon_own",
        scratch=[pltpu.SemaphoreType.DMA((sources,))],
        in_specs=[WHOLE, ANY],
        flops=2 * tokens * width * features,
        bytes_accessed=2 * sources * width * features,
    )
    dec = in_vmem(dec)
    keep, send = call(
        recon_rest,
        [shape((tokens, half + LANES), F32)] * 2,
        (total, pen, dec, *others),
        "recon_rest",
        flops=2 * tokens * width * features * (sources - 1),
        bytes_accessed=2 * (sources - 1) * width * features,
    )
    (msg,) = call(pair_sum, [shape((tokens, half + LANES), BF16)], (keep, swap(send, "feat", 1)), "pair_sum")
    bit = 2
    while bit < feats:
        pair = (bit, 2 * bit, 3 * bit) if 2 * bit < feats else (bit,)
        msgs = [msg] + [swap(msg, "feat", k) for k in pair]
        bit <<= len(pair) // 2 + 1
        if bit < feats:
            (msg,) = call(group_sum, [shape((tokens, half + LANES), BF16)], msgs, "group_sum")
    mine, own_rows, pen_all = call(
        functools.partial(error_half, rows),
        [shape((tokens + 8, half), BF16), shape((8, half), F32), shape((8, LANES), F32)],
        (targets, *msgs),
        "error_half",
    )
    recon, grad, score, part, *sends = call(
        functools.partial(act_grads, rows),
        [shape((rows, width), BF16), shape((tokens, width), BF16), shape((8, LANES), F32), shape((tokens, features), F32)]
        + [shape((tokens, features + LANES), BF16)] * (layers - 1),
        (mine, swap(mine, "feat", 1), own_rows, pen_all, dec),
        "act_grads",
        flops=2 * tokens * width * features * sources,
        bytes_accessed=2 * sources * width * features,
    )
    gots = [swap(sends[k - 1], "layer", k) for k in range(1, layers)]
    steps = max(1, features // 256)
    (dec_grad,) = call(
        functools.partial(decoder_grads, steps),
        [shape((sources, features, width), BF16)],
        (grad, acts, *others),
        "decoder_grads",
        scratch=[pltpu.VMEM((2, features // steps, width), BF16), pltpu.SemaphoreType.DMA((2,))],
        out_specs=[ANY],
        flops=2 * tokens * width * features * sources,
        bytes_accessed=2 * sources * width * features,
    )
    block = 256
    enc_grad, loss = pl.pallas_call(
        functools.partial(encoder_grad, layers * tokens * width),
        out_shape=[shape((width, features), BF16), shape((1, 1), F32)],
        grid=(width // block,),
        in_specs=[pl.BlockSpec((tokens, block), lambda i: (0, i))] + [WHOLE] * (3 + layers),
        out_specs=[pl.BlockSpec((block, features), lambda i: (i, 0)), pl.BlockSpec((1, 1), lambda i: (0, 0))],
        scratch_shapes=[pltpu.VMEM((tokens, features), BF16)],
        compiler_params=pltpu.CompilerParams(vmem_limit_bytes=16 * MIB),
        cost_estimate=pl.CostEstimate(flops=2 * tokens * width * features, bytes_accessed=2 * width * features, transcendentals=0),
        name="encoder_grad",
    )(x, part, gate, sparse, score, *gots)
    return loss[0, 0], recon[None], dec_grad[:, None], enc_grad[None]


def solution(mesh):
    return jax.shard_map(
        body,
        mesh=mesh,
        in_specs=(
            P("layer", "feat", None),
            P("layer", None, "feat"),
            P("layer", "feat"),
            P(None, "layer", "feat", None),
            P("layer", "feat", None),
        ),
        out_specs=(
            P(),
            P("layer", "feat", None),
            P(None, "layer", "feat", None),
            P("layer", None, "feat"),
        ),
        check_vma=False,
    )
```

```python
import functools

import jax
import jax.numpy as jnp
from jax import lax
from jax.experimental import pallas as pl
from jax.experimental.pallas import tpu as pltpu
from jax.sharding import PartitionSpec as P

ERROR_SCALE = 32.0
PENALTY_WEIGHT = 4.0
F32 = jnp.float32
BF16 = jnp.bfloat16
LANES = 128
MIB = 1 << 20
WHOLE = pl.BlockSpec(memory_space=pltpu.VMEM)
ANY = pl.BlockSpec(memory_space=pl.ANY)
NT = (((1,), (1,)), ((), ()))
TN = (((0,), (0,)), ((), ()))


def in_hbm(x):
    return pltpu.with_memory_space_constraint(x, pltpu.HBM)


def shape(dims, dtype):
    return jax.ShapeDtypeStruct(dims, dtype)


def call(body, outs, args, name, scratch=(), limit=16, in_specs=None, out_specs=None, flops=0, bytes_accessed=0):
    return pl.pallas_call(
        body,
        out_shape=outs,
        in_specs=in_specs or [WHOLE] * len(args),
        out_specs=out_specs or [WHOLE] * len(outs),
        scratch_shapes=list(scratch),
        compiler_params=pltpu.CompilerParams(vmem_limit_bytes=limit * MIB),
        cost_estimate=pl.CostEstimate(flops=flops, bytes_accessed=bytes_accessed, transcendentals=0),
        name=name,
    )(*args)


def swap(x, axis, bits):
    size = lax.axis_size(axis)
    return lax.ppermute(x, axis, [(i, i ^ bits) for i in range(size)])


def split3(value):
    high = value.astype(BF16)
    rest = value - high.astype(F32)
    middle = rest.astype(BF16)
    low = (rest - middle.astype(F32)).astype(BF16)
    return high, middle, low


def spread3(value, dims):
    high, middle, low = (part.astype(F32) for part in split3(value))
    lane = lax.broadcasted_iota(jnp.int32, dims, 1)
    block = jnp.where(lane == 0, high, jnp.where(lane == 1, middle, jnp.where(lane == 2, low, 0.0)))
    return block.astype(BF16)


def pack(res_hbm, target_hbm, thr_hbm, out_ref, cutoff_ref, res_ref, target_ref, thr_ref, sems):
    copies = [
        pltpu.make_async_copy(res_hbm, res_ref, sems.at[0]),
        pltpu.make_async_copy(target_hbm, target_ref, sems.at[1]),
        pltpu.make_async_copy(thr_hbm, thr_ref, sems.at[2]),
    ]
    for copy in copies:
        copy.start()
    for copy in copies:
        copy.wait()
    rows = res_ref.shape[0]
    out_ref[...] = jnp.zeros_like(out_ref)
    out_ref[:rows] = res_ref[...]
    out_ref[rows : 2 * rows] = target_ref[...]
    cutoff_ref[...] = (thr_ref[...].astype(F32) + 0.5) / 2048.0


def stack(*refs):
    out_ref = refs[-1]
    height = refs[0].shape[0]
    for i, ref in enumerate(refs[:-1]):
        out_ref[i * height : (i + 1) * height] = ref[...]


def gather_rows(rows, height, tokens, first, blocks):
    dims = (tokens, blocks.shape[0])
    token = lax.broadcasted_iota(jnp.int32, dims, 0)
    place = lax.broadcasted_iota(jnp.int32, dims, 1)
    row = place % height - first
    device = (place // height) ^ lax.axis_index("feat")
    chosen = (row >= 0) & (row < rows) & (device * rows + row == token)
    picked = jnp.dot(jnp.where(chosen, 1.0, 0.0).astype(BF16), blocks, preferred_element_type=F32)
    return picked.astype(BF16)


def encode(rows, height, *refs):
    *block_refs, enc_ref, cutoff_ref, x_ref, target_ref, acts_ref, gate_ref, sparse_ref, pen_ref = refs
    tokens = x_ref.shape[0]
    blocks = jnp.concatenate([ref[...] for ref in block_refs], axis=0)
    x = gather_rows(rows, height, tokens, 0, blocks)
    x_ref[...] = x
    target_ref[...] = gather_rows(rows, height, tokens, rows, blocks)
    preact = jnp.dot(x, enc_ref[...], preferred_element_type=F32)
    firing = preact > cutoff_ref[...]
    acts = jnp.where(firing, preact, 0.0).astype(BF16)
    acts_ref[...] = acts
    wide = acts.astype(F32)
    magnitude = jnp.sum(jnp.abs(wide), axis=0, keepdims=True) / tokens
    sign = jnp.where(wide > 0, 1.0, jnp.where(wide < 0, -1.0, 0.0))
    gate_ref[...] = firing.astype(F32)
    sparse_ref[...] = 2.0 * PENALTY_WEIGHT * magnitude * sign / tokens
    pen = jnp.sum(magnitude * magnitude, axis=1, keepdims=True)
    pen_ref[...] = jnp.broadcast_to(pen, pen_ref.shape)


def recon_own(acts_ref, dec_hbm, total_ref, buf, sems):
    me = lax.axis_index("layer")
    pieces = buf.shape[0]
    block = buf.shape[1]
    copies = []
    for i in range(pieces):
        copies.append(pltpu.make_async_copy(dec_hbm.at[me, pl.ds(i * block, block)], buf.at[i], sems.at[i]))
        copies[-1].start()
    total = jnp.zeros(total_ref.shape, F32)
    for i in range(pieces):
        copies[i].wait()
        total = total + jnp.dot(acts_ref[:, i * block : (i + 1) * block], buf[i], preferred_element_type=F32)
    total_ref[...] = total


def recon_rest(*refs):
    total_ref, pen_ref, dec_ref, *acts = refs[:-2]
    keep_ref, send_ref = refs[-2:]
    me = lax.axis_index("layer")
    half = dec_ref.shape[2] // 2
    total = total_ref[...]
    for k, acts_ref in enumerate(acts, 1):
        total = total + jnp.dot(acts_ref[...], dec_ref[me ^ k], preferred_element_type=F32)
    first, second = total[:, :half], total[:, half:]
    low = lax.axis_index("feat") % 2 == 0
    pen = jnp.broadcast_to(pen_ref[0:1, :], (total.shape[0], LANES))
    keep_ref[:, :half] = jnp.where(low, first, second)
    send_ref[:, :half] = jnp.where(low, second, first)
    keep_ref[:, half:] = pen
    send_ref[:, half:] = pen


def pair_sum(keep_ref, got_ref, msg_ref):
    half = keep_ref.shape[1] - LANES
    msg_ref[:, :half] = (keep_ref[:, :half] + got_ref[:, :half]).astype(BF16)
    pen = keep_ref[0:1, half : half + 1] + got_ref[0:1, half : half + 1]
    msg_ref[:, half:] = spread3(pen, (keep_ref.shape[0], LANES))


def sum_messages(refs):
    terms = [ref[...].astype(F32) for ref in refs]
    while len(terms) > 1:
        terms = [terms[i] + terms[i + 1] for i in range(0, len(terms), 2)]
    return terms[0]


def group_sum(*refs):
    half = refs[0].shape[1] - LANES
    total = sum_messages(refs[:-1])
    refs[-1][:, :half] = total[:, :half].astype(BF16)
    pen = jnp.sum(total[0:1, half:], axis=1, keepdims=True)
    refs[-1][:, half:] = spread3(pen, (total.shape[0], LANES))


def pick_rows(device, rows, tokens):
    row = lax.broadcasted_iota(jnp.int32, (8, tokens), 0)
    column = lax.broadcasted_iota(jnp.int32, (8, tokens), 1)
    return jnp.where((column == device * rows + row) & (row < rows), 1.0, 0.0).astype(BF16)


def error_half(rows, target_ref, *refs):
    *msgs, out_ref, own_ref, pen_ref = refs
    tokens, half = target_ref.shape[0], target_ref.shape[1] // 2
    me = lax.axis_index("feat")
    total = sum_messages(msgs)
    recon = total[:, :half]
    target = jnp.where(me % 2 == 0, target_ref[:, :half], target_ref[:, half:]).astype(F32)
    error = recon - target
    squares = jnp.sum(jnp.sum(error * error, axis=1, keepdims=True), axis=0, keepdims=True)
    narrow = recon.astype(BF16)
    own_ref[...] = jnp.dot(pick_rows(me, rows, tokens), narrow, preferred_element_type=F32)
    theirs = jnp.dot(pick_rows(me ^ 1, rows, tokens), narrow, preferred_element_type=F32)
    row = lax.broadcasted_iota(jnp.int32, (8, half), 0)
    parts = spread3(squares, (8, LANES)).astype(F32)
    parts = jnp.concatenate([parts, jnp.zeros((8, half - LANES), F32)], axis=1)
    out_ref[:tokens, :] = (error / ERROR_SCALE).astype(BF16)
    out_ref[tokens:, :] = jnp.where(row < rows, theirs, jnp.where(row == rows, parts, 0.0)).astype(BF16)
    pen = jnp.sum(total[0:1, half:], axis=1, keepdims=True)
    pen_ref[...] = jnp.broadcast_to(pen, pen_ref.shape)


def act_grads(rows, mine_ref, got_ref, own_ref, pen_ref, dec_ref, *outs):
    recon_ref, grad_ref, score_ref, part_ref, *msgs = outs
    tokens, half = grad_ref.shape[0], grad_ref.shape[1] // 2
    low = lax.axis_index("feat") % 2 == 0
    me = lax.axis_index("layer")
    first = jnp.where(low, mine_ref[:tokens, :], got_ref[:tokens, :])
    second = jnp.where(low, got_ref[:tokens, :], mine_ref[:tokens, :])
    grad_ref[:, :half] = first
    grad_ref[:, half:] = second
    extra = got_ref[tokens:, :].astype(F32)
    own = own_ref[...]
    recon_ref[:, :half] = jnp.where(low, own, extra)[:rows].astype(BF16)
    recon_ref[:, half:] = jnp.where(low, extra, own)[:rows].astype(BF16)
    mine_extra = mine_ref[tokens:, :].astype(F32)
    squares = jnp.sum(mine_extra[rows : rows + 1, :LANES], axis=1, keepdims=True)
    squares = squares + jnp.sum(extra[rows : rows + 1, :LANES], axis=1, keepdims=True)
    score = squares + 2.0 * ERROR_SCALE * PENALTY_WEIGHT * pen_ref[0:1, 0:1]
    score_ref[...] = jnp.broadcast_to(score, score_ref.shape)
    grad = grad_ref[...]
    width = dec_ref.shape[1]
    for k in range(len(msgs), -1, -1):
        part = lax.dot_general(dec_ref[me ^ k], grad, NT, preferred_element_type=F32).T
        if k:
            msgs[k - 1][:, :width] = part.astype(BF16)
            msgs[k - 1][:, width:] = spread3(score, (tokens, LANES))
        else:
            part_ref[...] = part


def decoder_grads(grad_ref, *refs):
    *acts, out_hbm, buf, sems = refs
    me = lax.axis_index("layer")
    block = buf.shape[1]
    steps = acts[0].shape[1] // block
    copies = []
    for k, acts_ref in enumerate(acts):
        turned = acts_ref[...].T
        for i in range(steps):
            n = len(copies)
            span = slice(i * block, (i + 1) * block)
            buf[n] = jnp.dot(turned[span], grad_ref[...], preferred_element_type=F32).astype(BF16)
            copies.append(pltpu.make_async_copy(buf.at[n], out_hbm.at[me ^ k, pl.ds(i * block, block)], sems.at[n]))
            copies[-1].start()
    for copy in copies:
        copy.wait()


def encoder_grad(count, x_ref, part_ref, gate_ref, sparse_ref, score_ref, *refs):
    *msgs, out_hbm, loss_ref, buf, sems = refs
    width = part_ref.shape[1]
    total = part_ref[...]
    for msg in msgs:
        total = total + msg[:, :width].astype(F32)
    pre = jnp.where(gate_ref[...] > 0, total + sparse_ref[...], 0.0).astype(BF16)
    turned = x_ref[...].T
    block = buf.shape[1]
    copies = []
    for i in range(buf.shape[0]):
        span = slice(i * block, (i + 1) * block)
        buf[i] = jnp.dot(turned[span], pre, preferred_element_type=F32).astype(BF16)
        copies.append(pltpu.make_async_copy(buf.at[i], out_hbm.at[pl.ds(i * block, block)], sems.at[i]))
        copies[-1].start()
    scores = [score_ref[0:1, 0:1]]
    for msg in msgs:
        scores.append(jnp.sum(msg[0:1, width:].astype(F32), axis=1, keepdims=True))
    while len(scores) > 1:
        scores = [scores[i] + scores[i + 1] for i in range(0, len(scores), 2)]
    loss_ref[...] = scores[0] / count
    for copy in copies:
        copy.wait()


def body(residual_in, enc_weight, thresholds, dec_weight, target):
    layers, feats = lax.axis_size("layer"), lax.axis_size("feat")
    rows, width = residual_in.shape[1:]
    features = enc_weight.shape[2]
    tokens, half = rows * feats, width // 2
    sources = dec_weight.shape[0]
    decoder = dec_weight[:, 0]

    height = -(-2 * rows // 8) * 8
    block, cutoff = call(
        pack,
        [shape((height, width), BF16), shape((1, features), F32)],
        (in_hbm(residual_in[0]), in_hbm(target[0]), in_hbm(thresholds)),
        "pack",
        scratch=[pltpu.VMEM((rows, width), BF16)] * 2 + [pltpu.VMEM((1, features), jnp.int32), pltpu.SemaphoreType.DMA((3,))],
        in_specs=[ANY] * 3,
        bytes_accessed=0,
    )
    blocks, bit = [block, swap(block, "feat", 1)], 2
    while bit < feats:
        (block,) = call(stack, [shape((bit * height, width), BF16)], blocks, "stack")
        pair = (bit, 2 * bit, 3 * bit) if 2 * bit < feats else (bit,)
        blocks = [block] + [swap(block, "feat", k) for k in pair]
        bit <<= len(pair) // 2 + 1
    x, targets, acts, gate, sparse, pen = call(
        functools.partial(encode, rows, height),
        [shape((tokens, width), BF16)] * 2
        + [shape((tokens, features), BF16), shape((tokens, features), F32), shape((tokens, features), F32), shape((8, LANES), F32)],
        (*blocks, enc_weight[0], cutoff),
        "encode",
        flops=2 * tokens * width * features,
        bytes_accessed=2 * width * features,
    )
    others = [swap(acts, "layer", k) for k in range(1, layers)]
    pieces = max(1, features // 256)
    (total,) = call(
        recon_own,
        [shape((tokens, width), F32)],
        (acts, in_hbm(decoder)),
        "recon_own",
        scratch=[pltpu.VMEM((pieces, features // pieces, width), BF16), pltpu.SemaphoreType.DMA((pieces,))],
        in_specs=[WHOLE, ANY],
        limit=12,
        flops=2 * tokens * width * features,
        bytes_accessed=2 * width * features,
    )
    keep, send = call(
        recon_rest,
        [shape((tokens, half + LANES), F32)] * 2,
        (total, pen, decoder, *others),
        "recon_rest",
        flops=2 * tokens * width * features * (sources - 1),
        bytes_accessed=2 * (sources - 1) * width * features,
    )
    (msg,) = call(pair_sum, [shape((tokens, half + LANES), BF16)], (keep, swap(send, "feat", 1)), "pair_sum")
    bit = 2
    while bit < feats:
        pair = (bit, 2 * bit, 3 * bit) if 2 * bit < feats else (bit,)
        msgs = [msg] + [swap(msg, "feat", k) for k in pair]
        bit <<= len(pair) // 2 + 1
        if bit < feats:
            (msg,) = call(group_sum, [shape((tokens, half + LANES), BF16)], msgs, "group_sum")
    mine, own_rows, pen_all = call(
        functools.partial(error_half, rows),
        [shape((tokens + 8, half), BF16), shape((8, half), F32), shape((8, LANES), F32)],
        (targets, *msgs),
        "error_half",
    )
    recon, grad, score, part, *sends = call(
        functools.partial(act_grads, rows),
        [shape((rows, width), BF16), shape((tokens, width), BF16), shape((8, LANES), F32), shape((tokens, features), F32)]
        + [shape((tokens, features + LANES), BF16)] * (layers - 1),
        (mine, swap(mine, "feat", 1), own_rows, pen_all, decoder),
        "act_grads",
        flops=2 * tokens * width * features * sources,
        bytes_accessed=2 * sources * width * features,
    )
    gots = [swap(sends[k - 1], "layer", k) for k in range(1, layers)]
    steps = max(1, features // 256)
    (dec_grad,) = call(
        decoder_grads,
        [shape((sources, features, width), BF16)],
        (grad, acts, *others),
        "decoder_grads",
        scratch=[pltpu.VMEM((sources * steps, features // steps, width), BF16), pltpu.SemaphoreType.DMA((sources * steps,))],
        limit=24,
        out_specs=[ANY],
        flops=2 * tokens * width * features * sources,
        bytes_accessed=2 * sources * width * features,
    )
    block = 256
    enc_grad, loss = call(
        functools.partial(encoder_grad, layers * tokens * width),
        [shape((width, features), BF16), shape((1, 1), F32)],
        (x, part, gate, sparse, score, *gots),
        "encoder_grad",
        scratch=[pltpu.VMEM((width // block, block, features), BF16), pltpu.SemaphoreType.DMA((width // block,))],
        out_specs=[ANY, WHOLE],
        flops=2 * tokens * width * features,
        bytes_accessed=2 * width * features,
    )
    return loss[0, 0], recon[None], dec_grad[:, None], enc_grad[None]


def solution(mesh):
    return jax.shard_map(
        body,
        mesh=mesh,
        in_specs=(
            P("layer", "feat", None),
            P("layer", None, "feat"),
            P("layer", "feat"),
            P(None, "layer", "feat", None),
            P("layer", "feat", None),
        ),
        out_specs=(
            P(),
            P("layer", "feat", None),
            P(None, "layer", "feat", None),
            P("layer", None, "feat"),
        ),
        check_vma=False,
    )
```

```python
import functools

import jax
import jax.numpy as jnp
from jax import lax
from jax.experimental import pallas as pl
from jax.experimental.pallas import tpu as pltpu
from jax.sharding import PartitionSpec as P

ERROR_SCALE = 32.0
PENALTY_WEIGHT = 4.0
F32 = jnp.float32
BF16 = jnp.bfloat16
LANES = 128
MIB = 1 << 20
WHOLE = pl.BlockSpec(memory_space=pltpu.VMEM)
ANY = pl.BlockSpec(memory_space=pl.ANY)
NT = (((1,), (1,)), ((), ()))
TN = (((0,), (0,)), ((), ()))


def in_hbm(x):
    return pltpu.with_memory_space_constraint(x, pltpu.HBM)


def shape(dims, dtype):
    return jax.ShapeDtypeStruct(dims, dtype)


def call(body, outs, args, name, scratch=(), limit=16, in_specs=None, out_specs=None, aliases=None, flops=0, bytes_accessed=0):
    return pl.pallas_call(
        body,
        out_shape=outs,
        in_specs=in_specs or [WHOLE] * len(args),
        out_specs=out_specs or [WHOLE] * len(outs),
        scratch_shapes=list(scratch),
        input_output_aliases=aliases or {},
        compiler_params=pltpu.CompilerParams(vmem_limit_bytes=limit * MIB),
        cost_estimate=pl.CostEstimate(flops=flops, bytes_accessed=bytes_accessed, transcendentals=0),
        name=name,
    )(*args)


def swap(x, axis, bits):
    size = lax.axis_size(axis)
    return lax.ppermute(x, axis, [(i, i ^ bits) for i in range(size)])


def split3(value):
    high = value.astype(BF16)
    rest = value - high.astype(F32)
    middle = rest.astype(BF16)
    low = (rest - middle.astype(F32)).astype(BF16)
    return high, middle, low


def spread3(value, dims):
    high, middle, low = (part.astype(F32) for part in split3(value))
    lane = lax.broadcasted_iota(jnp.int32, dims, 1)
    block = jnp.where(lane == 0, high, jnp.where(lane == 1, middle, jnp.where(lane == 2, low, 0.0)))
    return block.astype(BF16)


def load_own(res_hbm, target_hbm, thr_hbm, out_ref, cutoff_ref, res_ref, target_ref, thr_ref, sems):
    places = ((res_hbm, res_ref), (target_hbm, target_ref), (thr_hbm, thr_ref))
    copies = [pltpu.make_async_copy(*place, sems.at[i]) for i, place in enumerate(places)]
    for copy in copies:
        copy.start()
    rows = res_ref.shape[0]
    out_ref[...] = jnp.zeros_like(out_ref)
    for copy in copies:
        copy.wait()
    out_ref[:rows] = res_ref[...]
    out_ref[rows : 2 * rows] = target_ref[...]
    cutoff_ref[...] = (thr_ref[...].astype(F32) + 0.5) / 2048.0


def pack(own_ref, res_ref, target_ref, out_ref):
    height, rows = own_ref.shape[0], res_ref.shape[0]
    out_ref[:height] = own_ref[...]
    out_ref[height:] = jnp.zeros_like(own_ref)
    out_ref[height : height + rows] = res_ref[...]
    out_ref[height + rows : height + 2 * rows] = target_ref[...]


def stack(*refs):
    out_ref = refs[-1]
    height = refs[0].shape[0]
    for i, ref in enumerate(refs[:-1]):
        out_ref[i * height : (i + 1) * height] = ref[...]


def fetch(_, src_hbm, out_ref, sem):
    copy = pltpu.make_async_copy(src_hbm, out_ref, sem)
    copy.start()
    copy.wait()


def gather_rows(rows, height, tokens, first, blocks):
    dims = (tokens, blocks.shape[0])
    token = lax.broadcasted_iota(jnp.int32, dims, 0)
    place = lax.broadcasted_iota(jnp.int32, dims, 1)
    row = place % height - first
    device = (place // height) ^ lax.axis_index("feat")
    chosen = (row >= 0) & (row < rows) & (device * rows + row == token)
    picked = jnp.dot(jnp.where(chosen, 1.0, 0.0).astype(BF16), blocks, preferred_element_type=F32)
    return picked.astype(BF16)


def encode(rows, height, *refs):
    *block_refs, enc_ref, cutoff_ref, x_ref, target_ref, acts_ref, gate_ref, sparse_ref, pen_ref = refs
    tokens = x_ref.shape[0]
    blocks = jnp.concatenate([ref[...] for ref in block_refs], axis=0)
    x = gather_rows(rows, height, tokens, 0, blocks)
    x_ref[...] = x
    target_ref[...] = gather_rows(rows, height, tokens, rows, blocks)
    preact = jnp.dot(x, enc_ref[...], preferred_element_type=F32)
    firing = preact > cutoff_ref[...]
    acts = jnp.where(firing, preact, 0.0).astype(BF16)
    acts_ref[...] = acts
    wide = acts.astype(F32)
    magnitude = jnp.sum(jnp.abs(wide), axis=0, keepdims=True) / tokens
    sign = jnp.where(wide > 0, 1.0, jnp.where(wide < 0, -1.0, 0.0))
    gate_ref[...] = firing.astype(F32)
    sparse_ref[...] = 2.0 * PENALTY_WEIGHT * magnitude * sign / tokens
    pen = jnp.sum(magnitude * magnitude, axis=1, keepdims=True)
    pen_ref[...] = jnp.broadcast_to(pen, pen_ref.shape)


def recon_own(acts_ref, dec_hbm, total_ref, buf, sems):
    me = lax.axis_index("layer")
    pieces = buf.shape[0]
    block = buf.shape[1]
    copies = []
    for i in range(pieces):
        copies.append(pltpu.make_async_copy(dec_hbm.at[me, pl.ds(i * block, block)], buf.at[i], sems.at[i]))
        copies[-1].start()
    total = jnp.zeros(total_ref.shape, F32)
    for i in range(pieces):
        copies[i].wait()
        total = total + jnp.dot(acts_ref[:, i * block : (i + 1) * block], buf[i], preferred_element_type=F32)
    total_ref[...] = total


def recon_half(theirs, total_ref, pen_ref, dec_ref, *refs):
    *acts, out_ref = refs
    me = lax.axis_index("layer")
    half = dec_ref.shape[2] // 2
    span = pl.ds(pl.multiple_of((lax.axis_index("feat") + theirs) % 2 * half, half), half)
    total = total_ref[:, span]
    for k, acts_ref in enumerate(acts, 1):
        total = total + jnp.dot(acts_ref[...], dec_ref[me ^ k, :, span], preferred_element_type=F32)
    out_ref[:, :half] = total
    out_ref[:, half:] = jnp.broadcast_to(pen_ref[0:1, :], (total.shape[0], LANES))


def pair_sum(keep_ref, got_ref, msg_ref):
    half = keep_ref.shape[1] - LANES
    msg_ref[:, :half] = (keep_ref[:, :half] + got_ref[:, :half]).astype(BF16)
    pen = keep_ref[0:1, half : half + 1] + got_ref[0:1, half : half + 1]
    msg_ref[:, half:] = spread3(pen, (keep_ref.shape[0], LANES))


def sum_messages(refs):
    terms = [ref[...].astype(F32) for ref in refs]
    while len(terms) > 1:
        terms = [terms[i] + terms[i + 1] for i in range(0, len(terms), 2)]
    return terms[0]


def group_sum(*refs):
    half = refs[0].shape[1] - LANES
    total = sum_messages(refs[:-1])
    refs[-1][:, :half] = total[:, :half].astype(BF16)
    pen = jnp.sum(total[0:1, half:], axis=1, keepdims=True)
    refs[-1][:, half:] = spread3(pen, (total.shape[0], LANES))


def pick_rows(device, rows, tokens):
    row = lax.broadcasted_iota(jnp.int32, (8, tokens), 0)
    column = lax.broadcasted_iota(jnp.int32, (8, tokens), 1)
    return jnp.where((column == device * rows + row) & (row < rows), 1.0, 0.0).astype(BF16)


def error_half(rows, target_ref, *refs):
    *msgs, out_ref, own_ref, pen_ref = refs
    tokens, half = target_ref.shape[0], target_ref.shape[1] // 2
    me = lax.axis_index("feat")
    total = sum_messages(msgs)
    recon = total[:, :half]
    target = jnp.where(me % 2 == 0, target_ref[:, :half], target_ref[:, half:]).astype(F32)
    error = recon - target
    squares = jnp.sum(jnp.sum(error * error, axis=1, keepdims=True), axis=0, keepdims=True)
    narrow = recon.astype(BF16)
    own_ref[...] = jnp.dot(pick_rows(me, rows, tokens), narrow, preferred_element_type=F32)
    theirs = jnp.dot(pick_rows(me ^ 1, rows, tokens), narrow, preferred_element_type=F32)
    row = lax.broadcasted_iota(jnp.int32, (8, half), 0)
    parts = spread3(squares, (8, LANES)).astype(F32)
    parts = jnp.concatenate([parts, jnp.zeros((8, half - LANES), F32)], axis=1)
    out_ref[:tokens, :] = (error / ERROR_SCALE).astype(BF16)
    out_ref[tokens:, :] = jnp.where(row < rows, theirs, jnp.where(row == rows, parts, 0.0)).astype(BF16)
    pen = jnp.sum(total[0:1, half:], axis=1, keepdims=True)
    pen_ref[...] = jnp.broadcast_to(pen, pen_ref.shape)


def act_grad(grad, dec):
    return lax.dot_general(dec, grad, NT, preferred_element_type=F32).T


def act_half(grad, dec_ref, source, theirs):
    half = grad.shape[1]
    span = pl.ds(pl.multiple_of((lax.axis_index("feat") + theirs) % 2 * half, half), half)
    return act_grad(grad, dec_ref[source, :, span])


def act_first(mine_ref, dec_ref, *outs):
    tokens = outs[0].shape[0]
    me = lax.axis_index("layer")
    for k, out_ref in enumerate(outs, 1):
        out_ref[...] = act_half(mine_ref[:tokens, :], dec_ref, me ^ k, 0)


def act_second(rows, count, mine_ref, got_ref, own_ref, pen_ref, dec_ref, *refs):
    parts = refs[:count]
    recon_ref, grad_ref, score_ref, *msgs = refs[count:]
    tokens, half = grad_ref.shape[0], grad_ref.shape[1] // 2
    low = lax.axis_index("feat") % 2 == 0
    me = lax.axis_index("layer")
    mine, got = mine_ref[:tokens, :], got_ref[:tokens, :]
    extra = got_ref[tokens:, :].astype(F32)
    mine_extra = mine_ref[tokens:, :].astype(F32)
    squares = jnp.sum(mine_extra[rows : rows + 1, :LANES], axis=1, keepdims=True)
    squares = squares + jnp.sum(extra[rows : rows + 1, :LANES], axis=1, keepdims=True)
    score = squares + 2.0 * ERROR_SCALE * PENALTY_WEIGHT * pen_ref[0:1, 0:1]
    score_ref[...] = jnp.broadcast_to(score, score_ref.shape)
    width = dec_ref.shape[1]
    for k, (part_ref, msg) in enumerate(zip(parts, msgs), 1):
        msg[:, :width] = (part_ref[...] + act_half(got, dec_ref, me ^ k, 1)).astype(BF16)
        msg[:, width:] = spread3(score, (tokens, LANES))
    grad_ref[:, :half] = jnp.where(low, mine, got)
    grad_ref[:, half:] = jnp.where(low, got, mine)
    own = own_ref[...]
    recon_ref[:, :half] = jnp.where(low, own, extra)[:rows].astype(BF16)
    recon_ref[:, half:] = jnp.where(low, extra, own)[:rows].astype(BF16)


def write_decoder_grads(first, grad_ref, acts, out_hbm, buf, sems):
    me = lax.axis_index("layer")
    block = buf.shape[1]
    steps = acts[0].shape[1] // block
    copies = []
    for k, acts_ref in enumerate(acts, first):
        turned = acts_ref[...].T
        for i in range(steps):
            n = len(copies)
            span = slice(i * block, (i + 1) * block)
            buf[n] = jnp.dot(turned[span], grad_ref[...], preferred_element_type=F32).astype(BF16)
            copies.append(pltpu.make_async_copy(buf.at[n], out_hbm.at[me ^ k, pl.ds(i * block, block)], sems.at[n]))
            copies[-1].start()
    return copies


def first_grads(grad_ref, dec_ref, *refs):
    *acts, out_hbm, part_ref, buf, sems = refs
    copies = write_decoder_grads(0, grad_ref, acts, out_hbm, buf, sems)
    part_ref[...] = act_grad(grad_ref[...], dec_ref[lax.axis_index("layer")])
    for copy in copies:
        copy.wait()


def last_grads(count, first, last, grad_ref, x_ref, part_ref, gate_ref, sparse_ref, score_ref, *refs):
    *rest, _, dec_hbm, enc_hbm, loss_ref, dec_buf, dec_sems, enc_buf, enc_sems = refs
    acts, msgs = rest[:last], rest[last:]
    copies = write_decoder_grads(first, grad_ref, acts, dec_hbm, dec_buf, dec_sems)
    width = part_ref.shape[1]
    total = part_ref[...]
    for msg in msgs:
        total = total + msg[:, :width].astype(F32)
    pre = jnp.where(gate_ref[...] > 0, total + sparse_ref[...], 0.0).astype(BF16)
    turned = x_ref[...].T
    block = enc_buf.shape[1]
    for i in range(enc_buf.shape[0]):
        span = slice(i * block, (i + 1) * block)
        enc_buf[i] = jnp.dot(turned[span], pre, preferred_element_type=F32).astype(BF16)
        copies.append(pltpu.make_async_copy(enc_buf.at[i], enc_hbm.at[pl.ds(i * block, block)], enc_sems.at[i]))
        copies[-1].start()
    scores = [score_ref[0:1, 0:1]]
    for msg in msgs:
        scores.append(jnp.sum(msg[0:1, width:].astype(F32), axis=1, keepdims=True))
    while len(scores) > 1:
        scores = [scores[i] + scores[i + 1] for i in range(0, len(scores), 2)]
    loss_ref[...] = scores[0] / count
    for copy in copies:
        copy.wait()


def body(residual_in, enc_weight, thresholds, dec_weight, target):
    layers, feats = lax.axis_size("layer"), lax.axis_size("feat")
    rows, width = residual_in.shape[1:]
    features = enc_weight.shape[2]
    tokens, half = rows * feats, width // 2
    sources = dec_weight.shape[0]
    decoder = dec_weight[:, 0]

    height = -(-2 * rows // 8) * 8
    mine = (residual_in[0], target[0])
    own, cutoff = call(
        load_own,
        [shape((height, width), BF16), shape((1, features), F32)],
        [in_hbm(part) for part in (*mine, thresholds)],
        "load_own",
        scratch=[pltpu.VMEM((rows, width), BF16)] * 2 + [pltpu.VMEM((1, features), jnp.int32), pltpu.SemaphoreType.DMA((3,))],
        in_specs=[ANY] * 3,
        bytes_accessed=2 * width * features,
    )
    (block,) = call(pack, [shape((2 * height, width), BF16)], (own, *(swap(part, "feat", 1) for part in mine)), "pack")
    (encoder,) = call(
        fetch,
        [shape((width, features), BF16)],
        (block, in_hbm(enc_weight[0])),
        "fetch",
        scratch=[pltpu.SemaphoreType.DMA(())],
        in_specs=[ANY] * 2,
        bytes_accessed=4 * width * features,
    )
    blocks, bit = [block], 2
    while bit < feats:
        pair = (bit, 2 * bit, 3 * bit) if 2 * bit < feats else (bit,)
        blocks = [block] + [swap(block, "feat", k) for k in pair]
        bit <<= len(pair) // 2 + 1
        if bit < feats:
            (block,) = call(stack, [shape((bit * height, width), BF16)], blocks, "stack")
    x, targets, acts, gate, sparse, pen = call(
        functools.partial(encode, rows, height),
        [shape((tokens, width), BF16)] * 2
        + [shape((tokens, features), BF16), shape((tokens, features), F32), shape((tokens, features), F32), shape((8, LANES), F32)],
        (*blocks, encoder, cutoff),
        "encode",
        limit=48,
        flops=2 * tokens * width * features,
        bytes_accessed=2 * width * features,
    )
    others = [swap(acts, "layer", k) for k in range(1, layers)]
    pieces = max(1, features // 256)
    (total,) = call(
        recon_own,
        [shape((tokens, width), F32)],
        (acts, in_hbm(decoder)),
        "recon_own",
        scratch=[pltpu.VMEM((pieces, features // pieces, width), BF16), pltpu.SemaphoreType.DMA((pieces,))],
        in_specs=[WHOLE, ANY],
        limit=12,
        flops=2 * tokens * width * features,
        bytes_accessed=2 * width * features,
    )
    send, keep = (
        call(
            functools.partial(recon_half, theirs),
            [shape((tokens, half + LANES), F32)],
            (total, pen, decoder, *others),
            name,
            flops=tokens * width * features * (sources - 1),
            bytes_accessed=(sources - 1) * width * features,
        )[0]
        for theirs, name in ((1, "recon_send"), (0, "recon_keep"))
    )
    (msg,) = call(pair_sum, [shape((tokens, half + LANES), BF16)], (keep, swap(send, "feat", 1)), "pair_sum")
    bit = 2
    while bit < feats:
        pair = (bit, 2 * bit, 3 * bit) if 2 * bit < feats else (bit,)
        msgs = [msg] + [swap(msg, "feat", k) for k in pair]
        bit <<= len(pair) // 2 + 1
        if bit < feats:
            (msg,) = call(group_sum, [shape((tokens, half + LANES), BF16)], msgs, "group_sum")
    mine, own_rows, pen_all = call(
        functools.partial(error_half, rows),
        [shape((tokens + 8, half), BF16), shape((8, half), F32), shape((8, LANES), F32)],
        (targets, *msgs),
        "error_half",
    )
    parts = call(
        act_first,
        [shape((tokens, features), F32)] * (layers - 1),
        (mine, decoder),
        "act_first",
        flops=tokens * width * features * (sources - 1),
        bytes_accessed=(sources - 1) * width * features,
    )
    recon, grad, score, *sends = call(
        functools.partial(act_second, rows, layers - 1),
        [shape((rows, width), BF16), shape((tokens, width), BF16), shape((8, LANES), F32)]
        + [shape((tokens, features + LANES), BF16)] * (layers - 1),
        (mine, swap(mine, "feat", 1), own_rows, pen_all, decoder, *parts),
        "act_second",
        flops=tokens * width * features * (sources - 1),
        bytes_accessed=(sources - 1) * width * features,
    )
    gots = [swap(sends[k - 1], "layer", k) for k in range(1, layers)]
    first, steps, block = sources - 1, max(1, features // 128), 128
    last = sources - first
    dec_grad, part = call(
        first_grads,
        [shape((sources, features, width), BF16), shape((tokens, features), F32)],
        (grad, decoder, acts, *others[: first - 1]),
        "first_grads",
        scratch=[pltpu.VMEM((first * steps, features // steps, width), BF16), pltpu.SemaphoreType.DMA((first * steps,))],
        limit=24,
        out_specs=[ANY, WHOLE],
        flops=2 * tokens * width * features * (first + 1),
        bytes_accessed=2 * first * width * features,
    )
    args = (grad, x, part, gate, sparse, score, *others[first - 1 :], *gots, dec_grad)
    dec_grad, enc_grad, loss = call(
        functools.partial(last_grads, layers * tokens * width, first, last),
        [shape((sources, features, width), BF16), shape((width, features), BF16), shape((1, 1), F32)],
        args,
        "last_grads",
        scratch=[
            pltpu.VMEM((last * steps, features // steps, width), BF16),
            pltpu.SemaphoreType.DMA((last * steps,)),
            pltpu.VMEM((width // block, block, features), BF16),
            pltpu.SemaphoreType.DMA((width // block,)),
        ],
        in_specs=[WHOLE] * (len(args) - 1) + [ANY],
        out_specs=[ANY, ANY, WHOLE],
        limit=24,
        aliases={len(args) - 1: 0},
        flops=2 * tokens * width * features * (last + 1),
        bytes_accessed=2 * (last + 1) * width * features,
    )
    return loss[0, 0], recon[None], dec_grad[:, None], enc_grad[None]


def solution(mesh):
    return jax.shard_map(
        body,
        mesh=mesh,
        in_specs=(
            P("layer", "feat", None),
            P("layer", None, "feat"),
            P("layer", "feat"),
            P(None, "layer", "feat", None),
            P("layer", "feat", None),
        ),
        out_specs=(
            P(),
            P("layer", "feat", None),
            P(None, "layer", "feat", None),
            P("layer", None, "feat"),
        ),
        check_vma=False,
    )
```

```python
import functools

import jax
import jax.numpy as jnp
from jax import lax
from jax.experimental import pallas as pl
from jax.experimental.pallas import tpu as pltpu
from jax.sharding import PartitionSpec as P

ERROR_SCALE = 32.0
PENALTY_WEIGHT = 4.0
F32 = jnp.float32
BF16 = jnp.bfloat16
LANES = 128
MIB = 1 << 20
WHOLE = pl.BlockSpec(memory_space=pltpu.VMEM)
ANY = pl.BlockSpec(memory_space=pl.ANY)
NT = (((1,), (1,)), ((), ()))
TN = (((0,), (0,)), ((), ()))


def in_hbm(x):
    return pltpu.with_memory_space_constraint(x, pltpu.HBM)


def shape(dims, dtype):
    return jax.ShapeDtypeStruct(dims, dtype)


def call(body, outs, args, name, scratch=(), limit=16, in_specs=None, out_specs=None, aliases=None, flops=0, bytes_accessed=0):
    return pl.pallas_call(
        body,
        out_shape=outs,
        in_specs=in_specs or [WHOLE] * len(args),
        out_specs=out_specs or [WHOLE] * len(outs),
        scratch_shapes=list(scratch),
        input_output_aliases=aliases or {},
        compiler_params=pltpu.CompilerParams(vmem_limit_bytes=limit * MIB),
        cost_estimate=pl.CostEstimate(flops=flops, bytes_accessed=bytes_accessed, transcendentals=0),
        name=name,
    )(*args)


def swap(x, axis, bits):
    size = lax.axis_size(axis)
    return lax.ppermute(x, axis, [(i, i ^ bits) for i in range(size)])


def exchange_order(size):
    return (1, 3, 2) if size == 4 else tuple(range(1, size))


def split3(value):
    high = value.astype(BF16)
    rest = value - high.astype(F32)
    middle = rest.astype(BF16)
    low = (rest - middle.astype(F32)).astype(BF16)
    return high, middle, low


def spread3(value, dims):
    high, middle, low = (part.astype(F32) for part in split3(value))
    lane = lax.broadcasted_iota(jnp.int32, dims, 1)
    block = jnp.where(lane == 0, high, jnp.where(lane == 1, middle, jnp.where(lane == 2, low, 0.0)))
    return block.astype(BF16)


def load_own(res_hbm, target_hbm, thr_hbm, res_ref, target_ref, cutoff_ref, thr_ref, sems):
    places = ((res_hbm, res_ref), (target_hbm, target_ref), (thr_hbm, thr_ref))
    copies = [pltpu.make_async_copy(*place, sems.at[i]) for i, place in enumerate(places)]
    for copy in copies:
        copy.start()
    for copy in copies:
        copy.wait()
    cutoff_ref[...] = (thr_ref[...].astype(F32) + 0.5) / 2048.0


def pack(res_ref, target_ref, res_got_ref, target_got_ref, out_ref):
    rows, width = res_ref.shape
    half = width // 2
    low = lax.axis_index("feat") % 2 == 0
    out_ref[...] = jnp.zeros_like(out_ref)
    for start, res, target in ((0, res_ref, target_ref), (rows, res_got_ref, target_got_ref)):
        out_ref[start : start + rows, :width] = res[...]
        out_ref[start : start + rows, width:] = jnp.where(low, target[:, :half], target[:, half:])


def stack(*refs):
    out_ref = refs[-1]
    height = refs[0].shape[0]
    for i, ref in enumerate(refs[:-1]):
        out_ref[i * height : (i + 1) * height] = ref[...]


def fetch(_, src_hbm, out_ref, sem):
    copy = pltpu.make_async_copy(src_hbm, out_ref, sem)
    copy.start()
    copy.wait()


def gather_rows(rows, height, tokens, blocks):
    dims = (tokens, blocks.shape[0])
    token = lax.broadcasted_iota(jnp.int32, dims, 0)
    place = lax.broadcasted_iota(jnp.int32, dims, 1)
    inner = place % height
    second = (inner >= rows).astype(jnp.int32)
    device = (place // height * 2 + second) ^ lax.axis_index("feat")
    chosen = (inner < 2 * rows) & (device * rows + inner - second * rows == token)
    picked = jnp.dot(jnp.where(chosen, 1.0, 0.0).astype(BF16), blocks, preferred_element_type=F32)
    return picked.astype(BF16)


def encode(rows, height, *refs):
    *block_refs, enc_ref, cutoff_ref, x_ref, target_ref, acts_ref, gate_ref, sparse_ref, pen_ref = refs
    tokens = x_ref.shape[0]
    blocks = jnp.concatenate([ref[...] for ref in block_refs], axis=0)
    gathered = gather_rows(rows, height, tokens, blocks)
    x = gathered[:, : x_ref.shape[1]]
    x_ref[...] = x
    target_ref[...] = gathered[:, x_ref.shape[1] :]
    preact = jnp.dot(x, enc_ref[...], preferred_element_type=F32)
    firing = preact > cutoff_ref[...]
    acts = jnp.where(firing, preact, 0.0).astype(BF16)
    acts_ref[...] = acts
    wide = acts.astype(F32)
    magnitude = jnp.sum(jnp.abs(wide), axis=0, keepdims=True) / tokens
    sign = jnp.where(wide > 0, 1.0, jnp.where(wide < 0, -1.0, 0.0))
    gate_ref[...] = firing.astype(F32)
    sparse_ref[...] = 2.0 * PENALTY_WEIGHT * magnitude * sign / tokens
    pen = jnp.sum(magnitude * magnitude, axis=1, keepdims=True)
    pen_ref[...] = jnp.broadcast_to(pen, pen_ref.shape)


def recon_own(acts_ref, dec_hbm, total_ref, buf, sems):
    me = lax.axis_index("layer")
    pieces = buf.shape[0]
    block = buf.shape[1]
    copies = []
    for i in range(pieces):
        copies.append(pltpu.make_async_copy(dec_hbm.at[me, pl.ds(i * block, block)], buf.at[i], sems.at[i]))
        copies[-1].start()
    total = jnp.zeros(total_ref.shape, F32)
    for i in range(pieces):
        copies[i].wait()
        total = total + jnp.dot(acts_ref[:, i * block : (i + 1) * block], buf[i], preferred_element_type=F32)
    total_ref[...] = total


def recon_half(theirs, order, total_ref, pen_ref, dec_ref, *refs):
    *acts, out_ref = refs
    me = lax.axis_index("layer")
    half = dec_ref.shape[2] // 2
    span = pl.ds(pl.multiple_of((lax.axis_index("feat") + theirs) % 2 * half, half), half)
    total = total_ref[:, span]
    for k, acts_ref in zip(order, acts):
        total = total + jnp.dot(acts_ref[...], dec_ref[me ^ k, :, span], preferred_element_type=F32)
    out_ref[:, :half] = total
    out_ref[:, half:] = jnp.broadcast_to(pen_ref[0:1, :], (total.shape[0], LANES))


def pair_sum(keep_ref, got_ref, msg_ref):
    half = keep_ref.shape[1] - LANES
    msg_ref[:, :half] = (keep_ref[:, :half] + got_ref[:, :half]).astype(BF16)
    pen = keep_ref[0:1, half : half + 1] + got_ref[0:1, half : half + 1]
    msg_ref[:, half:] = spread3(pen, (keep_ref.shape[0], LANES))


def sum_messages(refs):
    terms = [ref[...].astype(F32) for ref in refs]
    while len(terms) > 1:
        terms = [terms[i] + terms[i + 1] for i in range(0, len(terms), 2)]
    return terms[0]


def group_sum(*refs):
    half = refs[0].shape[1] - LANES
    total = sum_messages(refs[:-1])
    refs[-1][:, :half] = total[:, :half].astype(BF16)
    pen = jnp.sum(total[0:1, half:], axis=1, keepdims=True)
    refs[-1][:, half:] = spread3(pen, (total.shape[0], LANES))


def pick_rows(device, rows, tokens):
    row = lax.broadcasted_iota(jnp.int32, (8, tokens), 0)
    column = lax.broadcasted_iota(jnp.int32, (8, tokens), 1)
    return jnp.where((column == device * rows + row) & (row < rows), 1.0, 0.0).astype(BF16)


def error_half(rows, target_ref, *refs):
    *msgs, out_ref, own_ref, pen_ref = refs
    tokens, half = target_ref.shape
    me = lax.axis_index("feat")
    total = sum_messages(msgs)
    recon = total[:, :half]
    error = recon - target_ref[...].astype(F32)
    squares = jnp.sum(jnp.sum(error * error, axis=1, keepdims=True), axis=0, keepdims=True)
    narrow = recon.astype(BF16)
    own_ref[...] = jnp.dot(pick_rows(me, rows, tokens), narrow, preferred_element_type=F32)
    theirs = jnp.dot(pick_rows(me ^ 1, rows, tokens), narrow, preferred_element_type=F32)
    row = lax.broadcasted_iota(jnp.int32, (8, half), 0)
    parts = spread3(squares, (8, LANES)).astype(F32)
    parts = jnp.concatenate([parts, jnp.zeros((8, half - LANES), F32)], axis=1)
    out_ref[:tokens, :] = (error / ERROR_SCALE).astype(BF16)
    out_ref[tokens:, :] = jnp.where(row < rows, theirs, jnp.where(row == rows, parts, 0.0)).astype(BF16)
    pen = jnp.sum(total[0:1, half:], axis=1, keepdims=True)
    pen_ref[...] = jnp.broadcast_to(pen, pen_ref.shape)


def act_grad(grad, dec):
    return lax.dot_general(dec, grad, NT, preferred_element_type=F32).T


def act_half(grad, dec_ref, source, theirs):
    half = grad.shape[1]
    span = pl.ds(pl.multiple_of((lax.axis_index("feat") + theirs) % 2 * half, half), half)
    return act_grad(grad, dec_ref[source, :, span])


def act_first(order, mine_ref, dec_ref, *outs):
    tokens = outs[0].shape[0]
    me = lax.axis_index("layer")
    for k, out_ref in zip(order, outs):
        out_ref[...] = act_half(mine_ref[:tokens, :], dec_ref, me ^ k, 0)


def act_second(rows, order, mine_ref, got_ref, pen_ref, dec_ref, *refs):
    parts = refs[: len(order)]
    grad_ref, score_ref, *msgs = refs[len(order) :]
    tokens, half = grad_ref.shape[0], grad_ref.shape[1] // 2
    low = lax.axis_index("feat") % 2 == 0
    me = lax.axis_index("layer")
    mine, got = mine_ref[:tokens, :], got_ref[:tokens, :]
    extra = got_ref[tokens:, :].astype(F32)
    mine_extra = mine_ref[tokens:, :].astype(F32)
    squares = jnp.sum(mine_extra[rows : rows + 1, :LANES], axis=1, keepdims=True)
    squares = squares + jnp.sum(extra[rows : rows + 1, :LANES], axis=1, keepdims=True)
    score = squares + 2.0 * ERROR_SCALE * PENALTY_WEIGHT * pen_ref[0:1, 0:1]
    score_ref[...] = jnp.broadcast_to(score, score_ref.shape)
    width = dec_ref.shape[1]
    for k, part_ref, msg in zip(order, parts, msgs):
        msg[:, :width] = (part_ref[...] + act_half(got, dec_ref, me ^ k, 1)).astype(BF16)
        msg[:, width:] = spread3(score, (tokens, LANES))
    grad_ref[:, :half] = jnp.where(low, mine, got)
    grad_ref[:, half:] = jnp.where(low, got, mine)


def write_decoder_grads(order, grad_ref, acts, out_hbm, buf, sems):
    me = lax.axis_index("layer")
    block = buf.shape[1]
    steps = acts[0].shape[1] // block
    copies = []
    for k, acts_ref in zip(order, acts):
        turned = acts_ref[...].T
        for i in range(steps):
            n = len(copies)
            span = slice(i * block, (i + 1) * block)
            buf[n] = jnp.dot(turned[span], grad_ref[...], preferred_element_type=F32).astype(BF16)
            copies.append(pltpu.make_async_copy(buf.at[n], out_hbm.at[me ^ k, pl.ds(i * block, block)], sems.at[n]))
            copies[-1].start()
    return copies


def first_grads(order, grad_ref, dec_ref, own_ref, got_ref, *refs):
    *acts, out_hbm, recon_hbm, part_ref, buf, sems, recon_ref, recon_sem = refs
    tokens, half = grad_ref.shape[0], grad_ref.shape[1] // 2
    low = lax.axis_index("feat") % 2 == 0
    own, extra = own_ref[...], got_ref[tokens:, :].astype(F32)
    rows = recon_ref.shape[0]
    recon_ref[:, :half] = jnp.where(low, own, extra)[:rows].astype(BF16)
    recon_ref[:, half:] = jnp.where(low, extra, own)[:rows].astype(BF16)
    copies = [pltpu.make_async_copy(recon_ref, recon_hbm, recon_sem)]
    copies[0].start()
    copies += write_decoder_grads(order, grad_ref, acts, out_hbm, buf, sems)
    part_ref[...] = act_grad(grad_ref[...], dec_ref[lax.axis_index("layer")])
    for copy in copies:
        copy.wait()


def last_grads(count, order, grad_ref, x_ref, part_ref, gate_ref, sparse_ref, score_ref, *refs):
    *rest, _, dec_hbm, enc_hbm, loss_hbm, dec_buf, dec_sems, enc_buf, enc_sems, loss_ref, loss_sem = refs
    acts, msgs = rest[: len(order)], rest[len(order) :]
    copies = write_decoder_grads(order, grad_ref, acts, dec_hbm, dec_buf, dec_sems)
    width = part_ref.shape[1]
    scores = [score_ref[0:1, 0:1]]
    for msg in msgs:
        scores.append(jnp.sum(msg[0:1, width:].astype(F32), axis=1, keepdims=True))
    while len(scores) > 1:
        scores = [scores[i] + scores[i + 1] for i in range(0, len(scores), 2)]
    loss_ref[...] = scores[0] / count
    copies.append(pltpu.make_async_copy(loss_ref, loss_hbm, loss_sem))
    copies[-1].start()
    total = part_ref[...]
    for msg in msgs:
        total = total + msg[:, :width].astype(F32)
    pre = jnp.where(gate_ref[...] > 0, total + sparse_ref[...], 0.0).astype(BF16)
    turned = x_ref[...].T
    block = enc_buf.shape[1]
    for i in range(enc_buf.shape[0]):
        span = slice(i * block, (i + 1) * block)
        enc_buf[i] = jnp.dot(turned[span], pre, preferred_element_type=F32).astype(BF16)
        copies.append(pltpu.make_async_copy(enc_buf.at[i], enc_hbm.at[pl.ds(i * block, block)], enc_sems.at[i]))
        copies[-1].start()
    for copy in copies:
        copy.wait()


def body(residual_in, enc_weight, thresholds, dec_weight, target):
    layers, feats = lax.axis_size("layer"), lax.axis_size("feat")
    rows, width = residual_in.shape[1:]
    features = enc_weight.shape[2]
    tokens, half = rows * feats, width // 2
    sources = dec_weight.shape[0]
    decoder = dec_weight[:, 0]

    height = -(-2 * rows // 8) * 8
    mine = (residual_in[0], target[0])
    *own, cutoff = call(
        load_own,
        [shape((rows, width), BF16)] * 2 + [shape((1, features), F32)],
        [in_hbm(part) for part in (*mine, thresholds)],
        "load_own",
        scratch=[pltpu.VMEM((1, features), jnp.int32), pltpu.SemaphoreType.DMA((3,))],
        in_specs=[ANY] * 3,
        bytes_accessed=2 * width * features,
    )
    got = [swap(part, "feat", 1) for part in mine]
    (block,) = call(pack, [shape((height, width + half), BF16)], (*own, *got), "pack")
    (encoder,) = call(
        fetch,
        [shape((width, features), BF16)],
        (block, in_hbm(enc_weight[0])),
        "fetch",
        scratch=[pltpu.SemaphoreType.DMA(())],
        in_specs=[ANY] * 2,
        bytes_accessed=4 * width * features,
    )
    blocks, bit = [block], 2
    while bit < feats:
        pair = (bit, 2 * bit, 3 * bit) if 2 * bit < feats else (bit,)
        blocks = [block] + [swap(block, "feat", k) for k in pair]
        bit <<= len(pair) // 2 + 1
        if bit < feats:
            (block,) = call(stack, [shape((bit // 2 * height, width + half), BF16)], blocks, "stack")
    x, targets, acts, gate, sparse, pen = call(
        functools.partial(encode, rows, height),
        [shape((tokens, width), BF16), shape((tokens, half), BF16)]
        + [shape((tokens, features), BF16), shape((tokens, features), F32), shape((tokens, features), F32), shape((8, LANES), F32)],
        (*blocks, encoder, cutoff),
        "encode",
        flops=2 * tokens * width * features,
        bytes_accessed=2 * width * features,
    )
    order = exchange_order(layers)
    others = [swap(acts, "layer", k) for k in order]
    pieces = max(1, features // 256)
    (total,) = call(
        recon_own,
        [shape((tokens, width), F32)],
        (acts, in_hbm(decoder)),
        "recon_own",
        scratch=[pltpu.VMEM((pieces, features // pieces, width), BF16), pltpu.SemaphoreType.DMA((pieces,))],
        in_specs=[WHOLE, ANY],
        limit=12,
        flops=2 * tokens * width * features,
        bytes_accessed=2 * width * features,
    )
    send, keep = (
        call(
            functools.partial(recon_half, theirs, order),
            [shape((tokens, half + LANES), F32)],
            (total, pen, decoder, *others),
            name,
            flops=tokens * width * features * (sources - 1),
            bytes_accessed=(sources - 1) * width * features,
        )[0]
        for theirs, name in ((1, "recon_send"), (0, "recon_keep"))
    )
    (msg,) = call(pair_sum, [shape((tokens, half + LANES), BF16)], (keep, swap(send, "feat", 1)), "pair_sum")
    bit = 2
    while bit < feats:
        pair = (bit, 2 * bit, 3 * bit) if 2 * bit < feats else (bit,)
        msgs = [msg] + [swap(msg, "feat", k) for k in pair]
        bit <<= len(pair) // 2 + 1
        if bit < feats:
            (msg,) = call(group_sum, [shape((tokens, half + LANES), BF16)], msgs, "group_sum")
    mine, own_rows, pen_all = call(
        functools.partial(error_half, rows),
        [shape((tokens + 8, half), BF16), shape((8, half), F32), shape((8, LANES), F32)],
        (targets, *msgs),
        "error_half",
    )
    back = (1, 3, 2) if layers == 4 else order
    parts = call(
        functools.partial(act_first, back),
        [shape((tokens, features), F32)] * (layers - 1),
        (mine, decoder),
        "act_first",
        flops=tokens * width * features * (sources - 1),
        bytes_accessed=(sources - 1) * width * features,
    )
    theirs = swap(mine, "feat", 1)
    grad, score, *sends = call(
        functools.partial(act_second, rows, back),
        [shape((tokens, width), BF16), shape((8, LANES), F32)] + [shape((tokens, features + LANES), BF16)] * (layers - 1),
        (mine, theirs, pen_all, decoder, *parts),
        "act_second",
        flops=tokens * width * features * (sources - 1),
        bytes_accessed=(sources - 1) * width * features,
    )
    gots = [swap(sends[back.index(k)], "layer", k) for k in (2, 3, 1)]
    first, steps, block = sources - 1, max(1, features // 128), 128
    last = sources - first
    dec_grad, recon, part = call(
        functools.partial(first_grads, (0, *order[: first - 1])),
        [shape((sources, features, width), BF16), shape((rows, width), BF16), shape((tokens, features), F32)],
        (grad, decoder, own_rows, theirs, acts, *others[: first - 1]),
        "first_grads",
        scratch=[pltpu.VMEM((first * steps, features // steps, width), BF16), pltpu.SemaphoreType.DMA((first * steps,))]
        + [pltpu.VMEM((rows, width), BF16), pltpu.SemaphoreType.DMA(())],
        limit=24,
        out_specs=[ANY, ANY, WHOLE],
        flops=2 * tokens * width * features * (first + 1),
        bytes_accessed=2 * first * width * features,
    )
    args = (grad, x, part, gate, sparse, score, *others[first - 1 :], *gots, dec_grad)
    dec_grad, enc_grad, loss = call(
        functools.partial(last_grads, layers * tokens * width, order[first - 1 :]),
        [shape((sources, features, width), BF16), shape((width, features), BF16), shape((1, 1), F32)],
        args,
        "last_grads",
        scratch=[
            pltpu.VMEM((last * steps, features // steps, width), BF16),
            pltpu.SemaphoreType.DMA((last * steps,)),
            pltpu.VMEM((width // block, block, features), BF16),
            pltpu.SemaphoreType.DMA((width // block,)),
            pltpu.VMEM((1, 1), F32),
            pltpu.SemaphoreType.DMA(()),
        ],
        in_specs=[WHOLE] * (len(args) - 1) + [ANY],
        out_specs=[ANY] * 3,
        limit=24,
        aliases={len(args) - 1: 0},
        flops=2 * tokens * width * features * (last + 1),
        bytes_accessed=2 * (last + 1) * width * features,
    )
    return loss[0, 0], recon[None], dec_grad[:, None], enc_grad[None]


def solution(mesh):
    return jax.shard_map(
        body,
        mesh=mesh,
        in_specs=(
            P("layer", "feat", None),
            P("layer", None, "feat"),
            P("layer", "feat"),
            P(None, "layer", "feat", None),
            P("layer", "feat", None),
        ),
        out_specs=(
            P(),
            P("layer", "feat", None),
            P(None, "layer", "feat", None),
            P("layer", None, "feat"),
        ),
        check_vma=False,
    )
```

```python
import functools

import jax
import jax.numpy as jnp
from jax import lax
from jax.experimental import pallas as pl
from jax.experimental.pallas import tpu as pltpu
from jax.sharding import PartitionSpec as P

ERROR_SCALE = 32.0
PENALTY_WEIGHT = 4.0
F32 = jnp.float32
BF16 = jnp.bfloat16
LANES = 128
MIB = 1 << 20
WHOLE = pl.BlockSpec(memory_space=pltpu.VMEM)
ANY = pl.BlockSpec(memory_space=pl.ANY)
NT = (((1,), (1,)), ((), ()))
TN = (((0,), (0,)), ((), ()))


def in_hbm(x):
    return pltpu.with_memory_space_constraint(x, pltpu.HBM)


def shape(dims, dtype):
    return jax.ShapeDtypeStruct(dims, dtype)


def call(body, outs, args, name, scratch=(), limit=16, in_specs=None, out_specs=None, aliases=None, flops=0, bytes_accessed=0):
    return pl.pallas_call(
        body,
        out_shape=outs,
        in_specs=in_specs or [WHOLE] * len(args),
        out_specs=out_specs or [WHOLE] * len(outs),
        scratch_shapes=list(scratch),
        input_output_aliases=aliases or {},
        compiler_params=pltpu.CompilerParams(vmem_limit_bytes=limit * MIB),
        cost_estimate=pl.CostEstimate(flops=flops, bytes_accessed=bytes_accessed, transcendentals=0),
        name=name,
    )(*args)


def swap(x, axis, bits):
    size = lax.axis_size(axis)
    return lax.ppermute(x, axis, [(i, i ^ bits) for i in range(size)])


def exchange_order(size):
    return (2, 3, 1) if size == 4 else tuple(range(1, size))


def split3(value):
    high = value.astype(BF16)
    rest = value - high.astype(F32)
    middle = rest.astype(BF16)
    low = (rest - middle.astype(F32)).astype(BF16)
    return high, middle, low


def spread3(value, dims):
    high, middle, low = (part.astype(F32) for part in split3(value))
    lane = lax.broadcasted_iota(jnp.int32, dims, 1)
    block = jnp.where(lane == 0, high, jnp.where(lane == 1, middle, jnp.where(lane == 2, low, 0.0)))
    return block.astype(BF16)


def load_own(res_hbm, target_hbm, thr_hbm, res_ref, target_ref, cutoff_ref, thr_ref, sems):
    places = ((res_hbm, res_ref), (target_hbm, target_ref), (thr_hbm, thr_ref))
    copies = [pltpu.make_async_copy(*place, sems.at[i]) for i, place in enumerate(places)]
    for copy in copies:
        copy.start()
    for copy in copies:
        copy.wait()
    cutoff_ref[...] = (thr_ref[...].astype(F32) + 0.5) / 2048.0


def pack(res_ref, target_ref, res_got_ref, target_got_ref, out_ref):
    rows, width = res_ref.shape
    half = width // 2
    low = lax.axis_index("feat") % 2 == 0
    out_ref[...] = jnp.zeros_like(out_ref)
    for start, res, target in ((0, res_ref, target_ref), (rows, res_got_ref, target_got_ref)):
        out_ref[start : start + rows, :width] = res[...]
        out_ref[start : start + rows, width:] = jnp.where(low, target[:, :half], target[:, half:])


def stack(*refs):
    out_ref = refs[-1]
    height = refs[0].shape[0]
    for i, ref in enumerate(refs[:-1]):
        out_ref[i * height : (i + 1) * height] = ref[...]


def fetch(_, src_hbm, out_ref, sem):
    copy = pltpu.make_async_copy(src_hbm, out_ref, sem)
    copy.start()
    copy.wait()


def gather_rows(rows, height, tokens, blocks):
    dims = (tokens, blocks.shape[0])
    token = lax.broadcasted_iota(jnp.int32, dims, 0)
    place = lax.broadcasted_iota(jnp.int32, dims, 1)
    inner = place % height
    second = (inner >= rows).astype(jnp.int32)
    device = (place // height * 2 + second) ^ lax.axis_index("feat")
    chosen = (inner < 2 * rows) & (device * rows + inner - second * rows == token)
    picked = jnp.dot(jnp.where(chosen, 1.0, 0.0).astype(BF16), blocks, preferred_element_type=F32)
    return picked.astype(BF16)


def encode(rows, height, *refs):
    *block_refs, enc_ref, cutoff_ref, x_ref, target_ref, acts_ref, gate_ref, sparse_ref, pen_ref = refs
    tokens = x_ref.shape[0]
    blocks = jnp.concatenate([ref[...] for ref in block_refs], axis=0)
    gathered = gather_rows(rows, height, tokens, blocks)
    x = gathered[:, : x_ref.shape[1]]
    x_ref[...] = x
    target_ref[...] = gathered[:, x_ref.shape[1] :]
    preact = jnp.dot(x, enc_ref[...], preferred_element_type=F32)
    firing = preact > cutoff_ref[...]
    acts = jnp.where(firing, preact, 0.0).astype(BF16)
    acts_ref[...] = acts
    wide = acts.astype(F32)
    magnitude = jnp.sum(jnp.abs(wide), axis=0, keepdims=True) / tokens
    sign = jnp.where(wide > 0, 1.0, jnp.where(wide < 0, -1.0, 0.0))
    gate_ref[...] = firing.astype(F32)
    sparse_ref[...] = 2.0 * PENALTY_WEIGHT * magnitude * sign / tokens
    pen = jnp.sum(magnitude * magnitude, axis=1, keepdims=True)
    pen_ref[...] = jnp.broadcast_to(pen, pen_ref.shape)


def recon_own(acts_ref, dec_hbm, total_ref, buf, sems):
    me = lax.axis_index("layer")
    pieces = buf.shape[0]
    block = buf.shape[1]
    copies = []
    for i in range(pieces):
        copies.append(pltpu.make_async_copy(dec_hbm.at[me, pl.ds(i * block, block)], buf.at[i], sems.at[i]))
        copies[-1].start()
    total = jnp.zeros(total_ref.shape, F32)
    for i in range(pieces):
        copies[i].wait()
        total = total + jnp.dot(acts_ref[:, i * block : (i + 1) * block], buf[i], preferred_element_type=F32)
    total_ref[...] = total


def recon_half(theirs, order, total_ref, pen_ref, dec_ref, *refs):
    *acts, out_ref = refs
    me = lax.axis_index("layer")
    half = dec_ref.shape[2] // 2
    span = pl.ds(pl.multiple_of((lax.axis_index("feat") + theirs) % 2 * half, half), half)
    total = total_ref[:, span]
    for k, acts_ref in zip(order, acts):
        total = total + jnp.dot(acts_ref[...], dec_ref[me ^ k, :, span], preferred_element_type=F32)
    out_ref[:, :half] = total
    out_ref[:, half:] = jnp.broadcast_to(pen_ref[0:1, :], (total.shape[0], LANES))


def pair_sum(keep_ref, got_ref, msg_ref):
    half = keep_ref.shape[1] - LANES
    msg_ref[:, :half] = (keep_ref[:, :half] + got_ref[:, :half]).astype(BF16)
    pen = keep_ref[0:1, half : half + 1] + got_ref[0:1, half : half + 1]
    msg_ref[:, half:] = spread3(pen, (keep_ref.shape[0], LANES))


def sum_messages(refs):
    terms = [ref[...].astype(F32) for ref in refs]
    while len(terms) > 1:
        terms = [terms[i] + terms[i + 1] for i in range(0, len(terms), 2)]
    return terms[0]


def group_sum(*refs):
    half = refs[0].shape[1] - LANES
    total = sum_messages(refs[:-1])
    refs[-1][:, :half] = total[:, :half].astype(BF16)
    pen = jnp.sum(total[0:1, half:], axis=1, keepdims=True)
    refs[-1][:, half:] = spread3(pen, (total.shape[0], LANES))


def pick_rows(device, rows, tokens):
    row = lax.broadcasted_iota(jnp.int32, (8, tokens), 0)
    column = lax.broadcasted_iota(jnp.int32, (8, tokens), 1)
    return jnp.where((column == device * rows + row) & (row < rows), 1.0, 0.0).astype(BF16)


def error_half(rows, target_ref, *refs):
    *msgs, out_ref, own_ref, pen_ref = refs
    tokens, half = target_ref.shape
    me = lax.axis_index("feat")
    total = sum_messages(msgs)
    recon = total[:, :half]
    error = recon - target_ref[...].astype(F32)
    squares = jnp.sum(jnp.sum(error * error, axis=1, keepdims=True), axis=0, keepdims=True)
    narrow = recon.astype(BF16)
    own_ref[...] = jnp.dot(pick_rows(me, rows, tokens), narrow, preferred_element_type=F32)
    theirs = jnp.dot(pick_rows(me ^ 1, rows, tokens), narrow, preferred_element_type=F32)
    row = lax.broadcasted_iota(jnp.int32, (8, half), 0)
    parts = spread3(squares, (8, LANES)).astype(F32)
    parts = jnp.concatenate([parts, jnp.zeros((8, half - LANES), F32)], axis=1)
    out_ref[:tokens, :] = (error / ERROR_SCALE).astype(BF16)
    out_ref[tokens:, :] = jnp.where(row < rows, theirs, jnp.where(row == rows, parts, 0.0)).astype(BF16)
    pen = jnp.sum(total[0:1, half:], axis=1, keepdims=True)
    pen_ref[...] = jnp.broadcast_to(pen, pen_ref.shape)


def act_grad(grad, dec):
    return lax.dot_general(dec, grad, NT, preferred_element_type=F32).T


def act_half(grad, dec_ref, source, theirs):
    half = grad.shape[1]
    span = pl.ds(pl.multiple_of((lax.axis_index("feat") + theirs) % 2 * half, half), half)
    return act_grad(grad, dec_ref[source, :, span])


def act_first(order, mine_ref, dec_ref, *outs):
    tokens = outs[0].shape[0]
    me = lax.axis_index("layer")
    for k, out_ref in zip(order, outs):
        out_ref[...] = act_half(mine_ref[:tokens, :], dec_ref, me ^ k, 0)


def act_second(rows, order, mine_ref, got_ref, pen_ref, dec_ref, *refs):
    parts = refs[: len(order)]
    grad_ref, score_ref, *msgs = refs[len(order) :]
    tokens, half = grad_ref.shape[0], grad_ref.shape[1] // 2
    low = lax.axis_index("feat") % 2 == 0
    me = lax.axis_index("layer")
    mine, got = mine_ref[:tokens, :], got_ref[:tokens, :]
    extra = got_ref[tokens:, :].astype(F32)
    mine_extra = mine_ref[tokens:, :].astype(F32)
    squares = jnp.sum(mine_extra[rows : rows + 1, :LANES], axis=1, keepdims=True)
    squares = squares + jnp.sum(extra[rows : rows + 1, :LANES], axis=1, keepdims=True)
    score = squares + 2.0 * ERROR_SCALE * PENALTY_WEIGHT * pen_ref[0:1, 0:1]
    score_ref[...] = jnp.broadcast_to(score, score_ref.shape)
    width = dec_ref.shape[1]
    for k, part_ref, msg in zip(order, parts, msgs):
        msg[:, :width] = (part_ref[...] + act_half(got, dec_ref, me ^ k, 1)).astype(BF16)
        msg[:, width:] = spread3(score, (tokens, LANES))
    grad_ref[:, :half] = jnp.where(low, mine, got)
    grad_ref[:, half:] = jnp.where(low, got, mine)


def write_decoder_grads(order, grad_ref, acts, out_hbm, buf, sems):
    me = lax.axis_index("layer")
    block = buf.shape[1]
    steps = acts[0].shape[1] // block
    copies = []
    for k, acts_ref in zip(order, acts):
        turned = acts_ref[...].T
        for i in range(steps):
            n = len(copies)
            span = slice(i * block, (i + 1) * block)
            buf[n] = jnp.dot(turned[span], grad_ref[...], preferred_element_type=F32).astype(BF16)
            copies.append(pltpu.make_async_copy(buf.at[n], out_hbm.at[me ^ k, pl.ds(i * block, block)], sems.at[n]))
            copies[-1].start()
    return copies


def first_grads(order, grad_ref, dec_ref, *refs):
    *acts, out_hbm, part_ref, buf, sems = refs
    copies = write_decoder_grads(order, grad_ref, acts, out_hbm, buf, sems)
    part_ref[...] = act_grad(grad_ref[...], dec_ref[lax.axis_index("layer")])
    for copy in copies:
        copy.wait()


def last_grads(count, order, grad_ref, own_ref, got_ref, x_ref, part_ref, gate_ref, sparse_ref, score_ref, *refs):
    *rest, _, dec_hbm, enc_hbm, loss_hbm, recon_hbm, dec_buf, dec_sems, enc_buf, enc_sems, loss_ref, loss_sem, recon_ref, recon_sem = refs
    acts, msgs = rest[: len(order)], rest[len(order) :]
    copies = write_decoder_grads(order, grad_ref, acts, dec_hbm, dec_buf, dec_sems)
    width = part_ref.shape[1]
    scores = [score_ref[0:1, 0:1]]
    for msg in msgs:
        scores.append(jnp.sum(msg[0:1, width:].astype(F32), axis=1, keepdims=True))
    while len(scores) > 1:
        scores = [scores[i] + scores[i + 1] for i in range(0, len(scores), 2)]
    loss_ref[...] = scores[0] / count
    copies.append(pltpu.make_async_copy(loss_ref, loss_hbm, loss_sem))
    copies[-1].start()
    total = part_ref[...]
    for msg in msgs:
        total = total + msg[:, :width].astype(F32)
    pre = jnp.where(gate_ref[...] > 0, total + sparse_ref[...], 0.0).astype(BF16)
    turned = x_ref[...].T
    block = enc_buf.shape[1]
    for i in range(enc_buf.shape[0]):
        span = slice(i * block, (i + 1) * block)
        enc_buf[i] = jnp.dot(turned[span], pre, preferred_element_type=F32).astype(BF16)
        copies.append(pltpu.make_async_copy(enc_buf.at[i], enc_hbm.at[pl.ds(i * block, block)], enc_sems.at[i]))
        copies[-1].start()
    tokens, half = grad_ref.shape[0], grad_ref.shape[1] // 2
    low = lax.axis_index("feat") % 2 == 0
    own, extra = own_ref[...], got_ref[tokens:, :].astype(F32)
    rows = recon_ref.shape[0]
    recon_ref[:, :half] = jnp.where(low, own, extra)[:rows].astype(BF16)
    recon_ref[:, half:] = jnp.where(low, extra, own)[:rows].astype(BF16)
    copies.append(pltpu.make_async_copy(recon_ref, recon_hbm, recon_sem))
    copies[-1].start()
    for copy in copies:
        copy.wait()


def body(residual_in, enc_weight, thresholds, dec_weight, target):
    layers, feats = lax.axis_size("layer"), lax.axis_size("feat")
    rows, width = residual_in.shape[1:]
    features = enc_weight.shape[2]
    tokens, half = rows * feats, width // 2
    sources = dec_weight.shape[0]
    decoder = dec_weight[:, 0]

    height = -(-2 * rows // 8) * 8
    mine = (residual_in[0], target[0])
    *own, cutoff = call(
        load_own,
        [shape((rows, width), BF16)] * 2 + [shape((1, features), F32)],
        [in_hbm(part) for part in (*mine, thresholds)],
        "load_own",
        scratch=[pltpu.VMEM((1, features), jnp.int32), pltpu.SemaphoreType.DMA((3,))],
        in_specs=[ANY] * 3,
        bytes_accessed=2 * width * features,
    )
    got = [swap(part, "feat", 1) for part in mine]
    (block,) = call(pack, [shape((height, width + half), BF16)], (*own, *got), "pack")
    (encoder,) = call(
        fetch,
        [shape((width, features), BF16)],
        (block, in_hbm(enc_weight[0])),
        "fetch",
        scratch=[pltpu.SemaphoreType.DMA(())],
        in_specs=[ANY] * 2,
        bytes_accessed=4 * width * features,
    )
    blocks, bit = [block], 2
    while bit < feats:
        pair = (bit, 2 * bit, 3 * bit) if 2 * bit < feats else (bit,)
        blocks = [block] + [swap(block, "feat", k) for k in pair]
        bit <<= len(pair) // 2 + 1
        if bit < feats:
            (block,) = call(stack, [shape((bit // 2 * height, width + half), BF16)], blocks, "stack")
    x, targets, acts, gate, sparse, pen = call(
        functools.partial(encode, rows, height),
        [shape((tokens, width), BF16), shape((tokens, half), BF16)]
        + [shape((tokens, features), BF16), shape((tokens, features), F32), shape((tokens, features), F32), shape((8, LANES), F32)],
        (*blocks, encoder, cutoff),
        "encode",
        flops=2 * tokens * width * features,
        bytes_accessed=2 * width * features,
    )
    back = exchange_order(layers)
    order = back[::-1]
    others = [swap(acts, "layer", k) for k in order]
    pieces = max(1, features // 256)
    (total,) = call(
        recon_own,
        [shape((tokens, width), F32)],
        (acts, in_hbm(decoder)),
        "recon_own",
        scratch=[pltpu.VMEM((pieces, features // pieces, width), BF16), pltpu.SemaphoreType.DMA((pieces,))],
        in_specs=[WHOLE, ANY],
        limit=12,
        flops=2 * tokens * width * features,
        bytes_accessed=2 * width * features,
    )
    send, keep = (
        call(
            functools.partial(recon_half, theirs, order),
            [shape((tokens, half + LANES), F32)],
            (total, pen, decoder, *others),
            name,
            flops=tokens * width * features * (sources - 1),
            bytes_accessed=(sources - 1) * width * features,
        )[0]
        for theirs, name in ((1, "recon_send"), (0, "recon_keep"))
    )
    (msg,) = call(pair_sum, [shape((tokens, half + LANES), BF16)], (keep, swap(send, "feat", 1)), "pair_sum")
    bit = 2
    while bit < feats:
        pair = (bit, 2 * bit, 3 * bit) if 2 * bit < feats else (bit,)
        msgs = [msg] + [swap(msg, "feat", k) for k in pair]
        bit <<= len(pair) // 2 + 1
        if bit < feats:
            (msg,) = call(group_sum, [shape((tokens, half + LANES), BF16)], msgs, "group_sum")
    mine, own_rows, pen_all = call(
        functools.partial(error_half, rows),
        [shape((tokens + 8, half), BF16), shape((8, half), F32), shape((8, LANES), F32)],
        (targets, *msgs),
        "error_half",
    )
    parts = call(
        functools.partial(act_first, back),
        [shape((tokens, features), F32)] * (layers - 1),
        (mine, decoder),
        "act_first",
        flops=tokens * width * features * (sources - 1),
        bytes_accessed=(sources - 1) * width * features,
    )
    theirs = swap(mine, "feat", 1)
    grad, score, *sends = call(
        functools.partial(act_second, rows, back),
        [shape((tokens, width), BF16), shape((8, LANES), F32)] + [shape((tokens, features + LANES), BF16)] * (layers - 1),
        (mine, theirs, pen_all, decoder, *parts),
        "act_second",
        flops=tokens * width * features * (sources - 1),
        bytes_accessed=(sources - 1) * width * features,
    )
    gots = [swap(send, "layer", k) for send, k in zip(sends, back)]
    first, steps, block = sources - 1, max(1, features // 128), 128
    last = sources - first
    dec_grad, part = call(
        functools.partial(first_grads, (0, *order[: first - 1])),
        [shape((sources, features, width), BF16), shape((tokens, features), F32)],
        (grad, decoder, acts, *others[: first - 1]),
        "first_grads",
        scratch=[pltpu.VMEM((first * steps, features // steps, width), BF16), pltpu.SemaphoreType.DMA((first * steps,))],
        limit=24,
        out_specs=[ANY, WHOLE],
        flops=2 * tokens * width * features * (first + 1),
        bytes_accessed=2 * first * width * features,
    )
    args = (grad, own_rows, theirs, x, part, gate, sparse, score, *others[first - 1 :], *gots, dec_grad)
    dec_grad, enc_grad, loss, recon = call(
        functools.partial(last_grads, layers * tokens * width, order[first - 1 :]),
        [shape((sources, features, width), BF16), shape((width, features), BF16), shape((1, 1), F32), shape((rows, width), BF16)],
        args,
        "last_grads",
        scratch=[
            pltpu.VMEM((last * steps, features // steps, width), BF16),
            pltpu.SemaphoreType.DMA((last * steps,)),
            pltpu.VMEM((width // block, block, features), BF16),
            pltpu.SemaphoreType.DMA((width // block,)),
            pltpu.VMEM((1, 1), F32),
            pltpu.SemaphoreType.DMA(()),
            pltpu.VMEM((rows, width), BF16),
            pltpu.SemaphoreType.DMA(()),
        ],
        in_specs=[WHOLE] * (len(args) - 1) + [ANY],
        out_specs=[ANY] * 4,
        limit=24,
        aliases={len(args) - 1: 0},
        flops=2 * tokens * width * features * (last + 1),
        bytes_accessed=2 * (last + 1) * width * features,
    )
    return loss[0, 0], recon[None], dec_grad[:, None], enc_grad[None]


def solution(mesh):
    return jax.shard_map(
        body,
        mesh=mesh,
        in_specs=(
            P("layer", "feat", None),
            P("layer", None, "feat"),
            P("layer", "feat"),
            P(None, "layer", "feat", None),
            P("layer", "feat", None),
        ),
        out_specs=(
            P(),
            P("layer", "feat", None),
            P(None, "layer", "feat", None),
            P("layer", None, "feat"),
        ),
        check_vma=False,
    )
```

```python
import functools

import jax
import jax.numpy as jnp
from jax import lax
from jax.experimental import pallas as pl
from jax.experimental.pallas import tpu as pltpu
from jax.sharding import PartitionSpec as P

ERROR_SCALE = 32.0
PENALTY_WEIGHT = 4.0
F32 = jnp.float32
BF16 = jnp.bfloat16
LANES = 128
MIB = 1 << 20
WHOLE = pl.BlockSpec(memory_space=pltpu.VMEM)
ANY = pl.BlockSpec(memory_space=pl.ANY)
NT = (((1,), (1,)), ((), ()))
TN = (((0,), (0,)), ((), ()))


def in_hbm(x):
    return pltpu.with_memory_space_constraint(x, pltpu.HBM)


def shape(dims, dtype):
    return jax.ShapeDtypeStruct(dims, dtype)


def call(body, outs, args, name, scratch=(), limit=16, in_specs=None, out_specs=None, aliases=None, flops=0, bytes_accessed=0):
    return pl.pallas_call(
        body,
        out_shape=outs,
        in_specs=in_specs or [WHOLE] * len(args),
        out_specs=out_specs or [WHOLE] * len(outs),
        scratch_shapes=list(scratch),
        input_output_aliases=aliases or {},
        compiler_params=pltpu.CompilerParams(vmem_limit_bytes=limit * MIB),
        cost_estimate=pl.CostEstimate(flops=flops, bytes_accessed=bytes_accessed, transcendentals=0),
        name=name,
    )(*args)


def swap(x, axis, bits):
    size = lax.axis_size(axis)
    return lax.ppermute(x, axis, [(i, i ^ bits) for i in range(size)])


def exchange_order(size):
    return (2, 3, 1) if size == 4 else tuple(range(1, size))


def split3(value):
    high = value.astype(BF16)
    rest = value - high.astype(F32)
    middle = rest.astype(BF16)
    low = (rest - middle.astype(F32)).astype(BF16)
    return high, middle, low


def spread3(value, dims):
    high, middle, low = (part.astype(F32) for part in split3(value))
    lane = lax.broadcasted_iota(jnp.int32, dims, 1)
    block = jnp.where(lane == 0, high, jnp.where(lane == 1, middle, jnp.where(lane == 2, low, 0.0)))
    return block.astype(BF16)


def load_own(res_hbm, target_hbm, thr_hbm, res_ref, target_ref, cutoff_ref, thr_ref, sems):
    places = ((res_hbm, res_ref), (target_hbm, target_ref), (thr_hbm, thr_ref))
    copies = [pltpu.make_async_copy(*place, sems.at[i]) for i, place in enumerate(places)]
    for copy in copies:
        copy.start()
    for copy in copies:
        copy.wait()
    cutoff_ref[...] = (thr_ref[...].astype(F32) + 0.5) / 2048.0


def pack(res_ref, target_ref, res_got_ref, target_got_ref, out_ref):
    rows, width = res_ref.shape
    half = width // 2
    low = lax.axis_index("feat") % 2 == 0
    out_ref[...] = jnp.zeros_like(out_ref)
    for start, res, target in ((0, res_ref, target_ref), (rows, res_got_ref, target_got_ref)):
        out_ref[start : start + rows, :width] = res[...]
        out_ref[start : start + rows, width:] = jnp.where(low, target[:, :half], target[:, half:])


def stack(*refs):
    out_ref = refs[-1]
    height = refs[0].shape[0]
    for i, ref in enumerate(refs[:-1]):
        out_ref[i * height : (i + 1) * height] = ref[...]


def fetch(_, src_hbm, out_ref, sem):
    copy = pltpu.make_async_copy(src_hbm, out_ref, sem)
    copy.start()
    copy.wait()


def gather_rows(rows, height, tokens, blocks):
    dims = (tokens, blocks.shape[0])
    token = lax.broadcasted_iota(jnp.int32, dims, 0)
    place = lax.broadcasted_iota(jnp.int32, dims, 1)
    inner = place % height
    second = (inner >= rows).astype(jnp.int32)
    device = (place // height * 2 + second) ^ lax.axis_index("feat")
    chosen = (inner < 2 * rows) & (device * rows + inner - second * rows == token)
    picked = jnp.dot(jnp.where(chosen, 1.0, 0.0).astype(BF16), blocks, preferred_element_type=F32)
    return picked.astype(BF16)


def encode(rows, height, *refs):
    *block_refs, enc_ref, cutoff_ref, x_ref, target_ref, acts_ref, gate_ref, sparse_ref, pen_ref = refs
    tokens = x_ref.shape[0]
    blocks = jnp.concatenate([ref[...] for ref in block_refs], axis=0)
    gathered = gather_rows(rows, height, tokens, blocks)
    x = gathered[:, : x_ref.shape[1]]
    x_ref[...] = x
    target_ref[...] = gathered[:, x_ref.shape[1] :]
    preact = jnp.dot(x, enc_ref[...], preferred_element_type=F32)
    firing = preact > cutoff_ref[...]
    acts = jnp.where(firing, preact, 0.0).astype(BF16)
    acts_ref[...] = acts
    wide = acts.astype(F32)
    magnitude = jnp.sum(jnp.abs(wide), axis=0, keepdims=True) / tokens
    sign = jnp.where(wide > 0, 1.0, jnp.where(wide < 0, -1.0, 0.0))
    gate_ref[...] = firing.astype(F32)
    sparse_ref[...] = 2.0 * PENALTY_WEIGHT * magnitude * sign / tokens
    pen = jnp.sum(magnitude * magnitude, axis=1, keepdims=True)
    pen_ref[...] = jnp.broadcast_to(pen, pen_ref.shape)


def recon_own(acts_ref, dec_hbm, total_ref, buf, sems):
    me = lax.axis_index("layer")
    pieces = buf.shape[0]
    block = buf.shape[1]
    copies = []
    for i in range(pieces):
        copies.append(pltpu.make_async_copy(dec_hbm.at[me, pl.ds(i * block, block)], buf.at[i], sems.at[i]))
        copies[-1].start()
    total = jnp.zeros(total_ref.shape, F32)
    for i in range(pieces):
        copies[i].wait()
        total = total + jnp.dot(acts_ref[:, i * block : (i + 1) * block], buf[i], preferred_element_type=F32)
    total_ref[...] = total


def recon_half(theirs, order, total_ref, pen_ref, dec_ref, *refs):
    *acts, out_ref = refs
    me = lax.axis_index("layer")
    half = dec_ref.shape[2] // 2
    span = pl.ds(pl.multiple_of((lax.axis_index("feat") + theirs) % 2 * half, half), half)
    total = total_ref[:, span]
    for k, acts_ref in zip(order, acts):
        total = total + jnp.dot(acts_ref[...], dec_ref[me ^ k, :, span], preferred_element_type=F32)
    out_ref[:, :half] = total
    out_ref[:, half:] = jnp.broadcast_to(pen_ref[0:1, :], (total.shape[0], LANES))


def pair_sum(keep_ref, got_ref, msg_ref):
    half = keep_ref.shape[1] - LANES
    for i in range(keep_ref.shape[0] // 8):
        rows, columns = slice(8 * i, 8 * i + 8), slice(i * half, (i + 1) * half)
        msg_ref[:, columns] = (keep_ref[rows, :half] + got_ref[rows, :half]).astype(BF16)
    pen = keep_ref[0:1, half : half + 1] + got_ref[0:1, half : half + 1]
    msg_ref[:, -LANES:] = spread3(pen, (8, LANES))


def sum_messages(refs):
    terms = [ref[...].astype(F32) for ref in refs]
    while len(terms) > 1:
        terms = [terms[i] + terms[i + 1] for i in range(0, len(terms), 2)]
    return terms[0]


def group_sum(*refs):
    total = sum_messages(refs[:-1])
    refs[-1][:, :-LANES] = total[:, :-LANES].astype(BF16)
    pen = jnp.sum(total[0:1, -LANES:], axis=1, keepdims=True)
    refs[-1][:, -LANES:] = spread3(pen, (8, LANES))


def pick_rows(device, rows, tokens):
    row = lax.broadcasted_iota(jnp.int32, (8, tokens), 0)
    column = lax.broadcasted_iota(jnp.int32, (8, tokens), 1)
    return jnp.where((column == device * rows + row) & (row < rows), 1.0, 0.0).astype(BF16)


def error_half(rows, target_ref, *refs):
    *msgs, out_ref, own_ref, pen_ref = refs
    tokens, half = target_ref.shape
    me = lax.axis_index("feat")
    total = sum_messages(msgs)
    recon = jnp.concatenate([total[:, i * half : (i + 1) * half] for i in range(tokens // 8)], axis=0)
    error = recon - target_ref[...].astype(F32)
    squares = jnp.sum(jnp.sum(error * error, axis=1, keepdims=True), axis=0, keepdims=True)
    narrow = recon.astype(BF16)
    own_ref[...] = jnp.dot(pick_rows(me, rows, tokens), narrow, preferred_element_type=F32)
    theirs = jnp.dot(pick_rows(me ^ 1, rows, tokens), narrow, preferred_element_type=F32)
    row = lax.broadcasted_iota(jnp.int32, (8, half), 0)
    parts = spread3(squares, (8, LANES)).astype(F32)
    parts = jnp.concatenate([parts, jnp.zeros((8, half - LANES), F32)], axis=1)
    out_ref[:tokens, :] = (error / ERROR_SCALE).astype(BF16)
    out_ref[tokens:, :] = jnp.where(row < rows, theirs, jnp.where(row == rows, parts, 0.0)).astype(BF16)
    pen = jnp.sum(total[0:1, -LANES:], axis=1, keepdims=True)
    pen_ref[...] = jnp.broadcast_to(pen, pen_ref.shape)


def act_grad(grad, dec):
    return lax.dot_general(dec, grad, NT, preferred_element_type=F32).T


def act_split(width):
    early = width // 2 // 256 * 256
    return early, width - early


def act_first(order, mine_ref, dec_ref, *outs):
    tokens, width = outs[0].shape[0], dec_ref.shape[2]
    early, late = act_split(width)
    side, me = lax.axis_index("feat") % 2, lax.axis_index("layer")
    span = pl.ds(pl.multiple_of(side * late, LANES), early)
    grad = jnp.where(side == 0, mine_ref[:tokens, :early], mine_ref[:tokens, width // 2 - early :])
    for k, out_ref in zip(order, outs):
        out_ref[...] = act_grad(grad, dec_ref[me ^ k, :, span])


def act_second(rows, order, mine_ref, got_ref, pen_ref, dec_ref, *refs):
    parts = refs[: len(order)]
    grad_ref, score_ref, *msgs = refs[len(order) :]
    tokens, half = grad_ref.shape[0], grad_ref.shape[1] // 2
    side, me = lax.axis_index("feat") % 2, lax.axis_index("layer")
    mine, got = mine_ref[:tokens, :], got_ref[:tokens, :]
    grad_ref[:, :half] = jnp.where(side == 0, mine, got)
    grad_ref[:, half:] = jnp.where(side == 0, got, mine)
    early, late = act_split(2 * half)
    span = pl.ds(pl.multiple_of((1 - side) * early, LANES), late)
    extra = got_ref[tokens:, :].astype(F32)
    mine_extra = mine_ref[tokens:, :].astype(F32)
    squares = jnp.sum(mine_extra[rows : rows + 1, :LANES], axis=1, keepdims=True)
    squares = squares + jnp.sum(extra[rows : rows + 1, :LANES], axis=1, keepdims=True)
    score = squares + 2.0 * ERROR_SCALE * PENALTY_WEIGHT * pen_ref[0:1, 0:1]
    score_ref[...] = jnp.broadcast_to(score, score_ref.shape)
    width = dec_ref.shape[1]
    for k, part_ref, msg in zip(order, parts, msgs):
        msg[:, :width] = (part_ref[...] + act_grad(grad_ref[:, span], dec_ref[me ^ k, :, span])).astype(BF16)
        msg[:, width:] = spread3(score, (tokens, LANES))


def write_decoder_grads(order, grad_ref, acts, out_hbm, buf, sems):
    me = lax.axis_index("layer")
    block = buf.shape[1]
    steps = acts[0].shape[1] // block
    copies = []
    for k, acts_ref in zip(order, acts):
        turned = acts_ref[...].T
        for i in range(steps):
            n = len(copies)
            span = slice(i * block, (i + 1) * block)
            buf[n] = jnp.dot(turned[span], grad_ref[...], preferred_element_type=F32).astype(BF16)
            copies.append(pltpu.make_async_copy(buf.at[n], out_hbm.at[me ^ k, pl.ds(i * block, block)], sems.at[n]))
            copies[-1].start()
    return copies


def first_grads(order, grad_ref, dec_ref, *refs):
    *acts, out_hbm, part_ref, buf, sems = refs
    copies = write_decoder_grads(order, grad_ref, acts, out_hbm, buf, sems)
    part_ref[...] = act_grad(grad_ref[...], dec_ref[lax.axis_index("layer")])
    for copy in copies:
        copy.wait()


def last_grads(count, order, grad_ref, own_ref, got_ref, x_ref, part_ref, gate_ref, sparse_ref, score_ref, *refs):
    *rest, _, dec_hbm, enc_hbm, loss_hbm, recon_hbm, dec_buf, dec_sems, enc_buf, enc_sems, loss_ref, loss_sem, recon_ref, recon_sem = refs
    acts, msgs = rest[: len(order)], rest[len(order) :]
    copies = []
    width = part_ref.shape[1]
    scores = [score_ref[0:1, 0:1]]
    for msg in msgs:
        scores.append(jnp.sum(msg[0:1, width:].astype(F32), axis=1, keepdims=True))
    while len(scores) > 1:
        scores = [scores[i] + scores[i + 1] for i in range(0, len(scores), 2)]
    loss_ref[...] = scores[0] / count
    copies.append(pltpu.make_async_copy(loss_ref, loss_hbm, loss_sem))
    copies[-1].start()
    total = part_ref[...]
    for msg in msgs:
        total = total + msg[:, :width].astype(F32)
    pre = jnp.where(gate_ref[...] > 0, total + sparse_ref[...], 0.0).astype(BF16)
    turned = x_ref[...].T
    block = enc_buf.shape[1]
    for i in range(enc_buf.shape[0]):
        span = slice(i * block, (i + 1) * block)
        enc_buf[i] = jnp.dot(turned[span], pre, preferred_element_type=F32).astype(BF16)
        copies.append(pltpu.make_async_copy(enc_buf.at[i], enc_hbm.at[pl.ds(i * block, block)], enc_sems.at[i]))
        copies[-1].start()
    copies += write_decoder_grads(order, grad_ref, acts, dec_hbm, dec_buf, dec_sems)
    tokens, half = grad_ref.shape[0], grad_ref.shape[1] // 2
    low = lax.axis_index("feat") % 2 == 0
    own, extra = own_ref[...], got_ref[tokens:, :].astype(F32)
    rows = recon_ref.shape[0]
    recon_ref[:, :half] = jnp.where(low, own, extra)[:rows].astype(BF16)
    recon_ref[:, half:] = jnp.where(low, extra, own)[:rows].astype(BF16)
    copies.append(pltpu.make_async_copy(recon_ref, recon_hbm, recon_sem))
    copies[-1].start()
    for copy in copies:
        copy.wait()


def body(residual_in, enc_weight, thresholds, dec_weight, target):
    layers, feats = lax.axis_size("layer"), lax.axis_size("feat")
    rows, width = residual_in.shape[1:]
    features = enc_weight.shape[2]
    tokens, half = rows * feats, width // 2
    sources = dec_weight.shape[0]
    decoder = dec_weight[:, 0]

    height = -(-2 * rows // 8) * 8
    mine = (residual_in[0], target[0])
    *own, cutoff = call(
        load_own,
        [shape((rows, width), BF16)] * 2 + [shape((1, features), F32)],
        [in_hbm(part) for part in (*mine, thresholds)],
        "load_own",
        scratch=[pltpu.VMEM((1, features), jnp.int32), pltpu.SemaphoreType.DMA((3,))],
        in_specs=[ANY] * 3,
        bytes_accessed=2 * width * features,
    )
    got = [swap(part, "feat", 1) for part in mine]
    (block,) = call(pack, [shape((height, width + half), BF16)], (*own, *got), "pack")
    (encoder,) = call(
        fetch,
        [shape((width, features), BF16)],
        (block, in_hbm(enc_weight[0])),
        "fetch",
        scratch=[pltpu.SemaphoreType.DMA(())],
        in_specs=[ANY] * 2,
        bytes_accessed=4 * width * features,
    )
    blocks, bit = [block], 2
    while bit < feats:
        pair = (bit, 2 * bit, 3 * bit) if 2 * bit < feats else (bit,)
        blocks = [block] + [swap(block, "feat", k) for k in pair]
        bit <<= len(pair) // 2 + 1
        if bit < feats:
            (block,) = call(stack, [shape((bit // 2 * height, width + half), BF16)], blocks, "stack")
    x, targets, acts, gate, sparse, pen = call(
        functools.partial(encode, rows, height),
        [shape((tokens, width), BF16), shape((tokens, half), BF16)]
        + [shape((tokens, features), BF16), shape((tokens, features), F32), shape((tokens, features), F32), shape((8, LANES), F32)],
        (*blocks, encoder, cutoff),
        "encode",
        flops=2 * tokens * width * features,
        bytes_accessed=2 * width * features,
    )
    back = exchange_order(layers)
    order = back[::-1]
    others = [swap(acts, "layer", k) for k in order]
    pieces = max(1, features // 256)
    (total,) = call(
        recon_own,
        [shape((tokens, width), F32)],
        (acts, in_hbm(decoder)),
        "recon_own",
        scratch=[pltpu.VMEM((pieces, features // pieces, width), BF16), pltpu.SemaphoreType.DMA((pieces,))],
        in_specs=[WHOLE, ANY],
        limit=12,
        flops=2 * tokens * width * features,
        bytes_accessed=2 * width * features,
    )
    send, keep = (
        call(
            functools.partial(recon_half, theirs, order),
            [shape((tokens, half + LANES), F32)],
            (total, pen, decoder, *others),
            name,
            flops=tokens * width * features * (sources - 1),
            bytes_accessed=(sources - 1) * width * features,
        )[0]
        for theirs, name in ((1, "recon_send"), (0, "recon_keep"))
    )
    (msg,) = call(pair_sum, [shape((8, tokens // 8 * half + LANES), BF16)], (keep, swap(send, "feat", 1)), "pair_sum")
    bit = 2
    while bit < feats:
        pair = (bit, 2 * bit, 3 * bit) if 2 * bit < feats else (bit,)
        msgs = [msg] + [swap(msg, "feat", k) for k in pair]
        bit <<= len(pair) // 2 + 1
        if bit < feats:
            (msg,) = call(group_sum, [shape(msg.shape, BF16)], msgs, "group_sum")
    mine, own_rows, pen_all = call(
        functools.partial(error_half, rows),
        [shape((tokens + 8, half), BF16), shape((8, half), F32), shape((8, LANES), F32)],
        (targets, *msgs),
        "error_half",
    )
    parts = call(
        functools.partial(act_first, back),
        [shape((tokens, features), F32)] * (layers - 1),
        (mine, decoder),
        "act_first",
        flops=tokens * width * features * (sources - 1),
        bytes_accessed=(sources - 1) * width * features,
    )
    theirs = swap(mine, "feat", 1)
    grad, score, *sends = call(
        functools.partial(act_second, rows, back),
        [shape((tokens, width), BF16), shape((8, LANES), F32)] + [shape((tokens, features + LANES), BF16)] * (layers - 1),
        (mine, theirs, pen_all, decoder, *parts),
        "act_second",
        flops=tokens * width * features * (sources - 1),
        bytes_accessed=(sources - 1) * width * features,
    )
    gots = [swap(send, "layer", k) for send, k in zip(sends, back)]
    first, steps, block = sources - 1, max(1, features // 128), 128
    last = sources - first
    dec_grad, part = call(
        functools.partial(first_grads, (0, *order[: first - 1])),
        [shape((sources, features, width), BF16), shape((tokens, features), F32)],
        (grad, decoder, acts, *others[: first - 1]),
        "first_grads",
        scratch=[pltpu.VMEM((first * steps, features // steps, width), BF16), pltpu.SemaphoreType.DMA((first * steps,))],
        limit=24,
        out_specs=[ANY, WHOLE],
        flops=2 * tokens * width * features * (first + 1),
        bytes_accessed=2 * first * width * features,
    )
    args = (grad, own_rows, theirs, x, part, gate, sparse, score, *others[first - 1 :], *gots, dec_grad)
    dec_grad, enc_grad, loss, recon = call(
        functools.partial(last_grads, layers * tokens * width, order[first - 1 :]),
        [shape((sources, features, width), BF16), shape((width, features), BF16), shape((1, 1), F32), shape((rows, width), BF16)],
        args,
        "last_grads",
        scratch=[
            pltpu.VMEM((last * steps, features // steps, width), BF16),
            pltpu.SemaphoreType.DMA((last * steps,)),
            pltpu.VMEM((width // block, block, features), BF16),
            pltpu.SemaphoreType.DMA((width // block,)),
            pltpu.VMEM((1, 1), F32),
            pltpu.SemaphoreType.DMA(()),
            pltpu.VMEM((rows, width), BF16),
            pltpu.SemaphoreType.DMA(()),
        ],
        in_specs=[WHOLE] * (len(args) - 1) + [ANY],
        out_specs=[ANY] * 4,
        limit=24,
        aliases={len(args) - 1: 0},
        flops=2 * tokens * width * features * (last + 1),
        bytes_accessed=2 * (last + 1) * width * features,
    )
    return loss[0, 0], recon[None], dec_grad[:, None], enc_grad[None]


def solution(mesh):
    return jax.shard_map(
        body,
        mesh=mesh,
        in_specs=(
            P("layer", "feat", None),
            P("layer", None, "feat"),
            P("layer", "feat"),
            P(None, "layer", "feat", None),
            P("layer", "feat", None),
        ),
        out_specs=(
            P(),
            P("layer", "feat", None),
            P(None, "layer", "feat", None),
            P("layer", None, "feat"),
        ),
        check_vma=False,
    )
```

```python
import functools

import jax
import jax.numpy as jnp
from jax import lax
from jax.experimental import pallas as pl
from jax.experimental.pallas import tpu as pltpu
from jax.sharding import PartitionSpec as P

ERROR_SCALE = 32.0
PENALTY_WEIGHT = 4.0
F32 = jnp.float32
BF16 = jnp.bfloat16
LANES = 128
MIB = 1 << 20
WHOLE = pl.BlockSpec(memory_space=pltpu.VMEM)
ANY = pl.BlockSpec(memory_space=pl.ANY)
NT = (((1,), (1,)), ((), ()))
TN = (((0,), (0,)), ((), ()))


def in_hbm(x):
    return pltpu.with_memory_space_constraint(x, pltpu.HBM)


def shape(dims, dtype):
    return jax.ShapeDtypeStruct(dims, dtype)


def call(body, outs, args, name, scratch=(), limit=16, in_specs=None, out_specs=None, aliases=None, flops=0, bytes_accessed=0):
    return pl.pallas_call(
        body,
        out_shape=outs,
        in_specs=in_specs or [WHOLE] * len(args),
        out_specs=out_specs or [WHOLE] * len(outs),
        scratch_shapes=list(scratch),
        input_output_aliases=aliases or {},
        compiler_params=pltpu.CompilerParams(vmem_limit_bytes=limit * MIB),
        cost_estimate=pl.CostEstimate(flops=flops, bytes_accessed=bytes_accessed, transcendentals=0),
        name=name,
    )(*args)


def swap(x, axis, bits):
    size = lax.axis_size(axis)
    return lax.ppermute(x, axis, [(i, i ^ bits) for i in range(size)])


def exchange_order(size):
    return (2, 3, 1) if size == 4 else tuple(range(1, size))


def split3(value):
    high = value.astype(BF16)
    rest = value - high.astype(F32)
    middle = rest.astype(BF16)
    low = (rest - middle.astype(F32)).astype(BF16)
    return high, middle, low


def spread3(value, dims):
    high, middle, low = (part.astype(F32) for part in split3(value))
    lane = lax.broadcasted_iota(jnp.int32, dims, 1)
    block = jnp.where(lane == 0, high, jnp.where(lane == 1, middle, jnp.where(lane == 2, low, 0.0)))
    return block.astype(BF16)


def load_own(res_hbm, target_hbm, thr_hbm, res_ref, target_ref, cutoff_ref, thr_ref, sems):
    places = ((res_hbm, res_ref), (target_hbm, target_ref), (thr_hbm, thr_ref))
    copies = [pltpu.make_async_copy(*place, sems.at[i]) for i, place in enumerate(places)]
    for copy in copies:
        copy.start()
    for copy in copies:
        copy.wait()
    cutoff_ref[...] = (thr_ref[...].astype(F32) + 0.5) / 2048.0


def pack(res_ref, target_ref, res_got_ref, target_got_ref, out_ref):
    rows, width = res_ref.shape
    half = width // 2
    low = lax.axis_index("feat") % 2 == 0
    out_ref[...] = jnp.zeros_like(out_ref)
    for start, res, target in ((0, res_ref, target_ref), (rows, res_got_ref, target_got_ref)):
        out_ref[start : start + rows, :width] = res[...]
        out_ref[start : start + rows, width:] = jnp.where(low, target[:, :half], target[:, half:])


def stack(*refs):
    out_ref = refs[-1]
    height = refs[0].shape[0]
    for i, ref in enumerate(refs[:-1]):
        out_ref[i * height : (i + 1) * height] = ref[...]


def fetch(_, src_hbm, out_ref, sem):
    copy = pltpu.make_async_copy(src_hbm, out_ref, sem)
    copy.start()
    copy.wait()


def gather_rows(rows, height, tokens, blocks):
    dims = (tokens, blocks.shape[0])
    token = lax.broadcasted_iota(jnp.int32, dims, 0)
    place = lax.broadcasted_iota(jnp.int32, dims, 1)
    inner = place % height
    second = (inner >= rows).astype(jnp.int32)
    device = (place // height * 2 + second) ^ lax.axis_index("feat")
    chosen = (inner < 2 * rows) & (device * rows + inner - second * rows == token)
    picked = jnp.dot(jnp.where(chosen, 1.0, 0.0).astype(BF16), blocks, preferred_element_type=F32)
    return picked.astype(BF16)


def encode(rows, height, *refs):
    *block_refs, enc_ref, cutoff_ref, x_ref, target_ref, acts_ref, gate_ref = refs
    tokens = x_ref.shape[0]
    blocks = jnp.concatenate([ref[...] for ref in block_refs], axis=0)
    gathered = gather_rows(rows, height, tokens, blocks)
    x = gathered[:, : x_ref.shape[1]]
    x_ref[...] = x
    target_ref[...] = gathered[:, x_ref.shape[1] :]
    preact = jnp.dot(x, enc_ref[...], preferred_element_type=F32)
    firing = preact > cutoff_ref[...]
    acts = jnp.where(firing, preact, 0.0).astype(BF16)
    acts_ref[...] = acts
    gate_ref[...] = firing.astype(F32)


def recon_own(acts_ref, dec_hbm, total_ref, sparse_ref, pen_ref, buf, sems):
    me = lax.axis_index("layer")
    pieces = buf.shape[0]
    block = buf.shape[1]
    copies = []
    for i in range(pieces):
        copies.append(pltpu.make_async_copy(dec_hbm.at[me, pl.ds(i * block, block)], buf.at[i], sems.at[i]))
        copies[-1].start()
    tokens = acts_ref.shape[0]
    wide = acts_ref[...].astype(F32)
    magnitude = jnp.sum(jnp.abs(wide), axis=0, keepdims=True) / tokens
    sign = jnp.where(wide > 0, 1.0, jnp.where(wide < 0, -1.0, 0.0))
    sparse_ref[...] = 2.0 * PENALTY_WEIGHT * magnitude * sign / tokens
    pen = jnp.sum(magnitude * magnitude, axis=1, keepdims=True)
    pen_ref[...] = jnp.broadcast_to(pen, pen_ref.shape)
    total = jnp.zeros(total_ref.shape, F32)
    for i in range(pieces):
        copies[i].wait()
        total = total + jnp.dot(acts_ref[:, i * block : (i + 1) * block], buf[i], preferred_element_type=F32)
    total_ref[...] = total


def recon_half(theirs, order, total_ref, pen_ref, dec_ref, *refs):
    *acts, out_ref = refs
    me = lax.axis_index("layer")
    half = dec_ref.shape[2] // 2
    span = pl.ds(pl.multiple_of((lax.axis_index("feat") + theirs) % 2 * half, half), half)
    total = total_ref[:, span]
    for k, acts_ref in zip(order, acts):
        total = total + jnp.dot(acts_ref[...], dec_ref[me ^ k, :, span], preferred_element_type=F32)
    out_ref[:, :half] = total
    out_ref[:, half:] = jnp.broadcast_to(pen_ref[0:1, :], (total.shape[0], LANES))


def pair_sum(keep_ref, got_ref, msg_ref):
    half = keep_ref.shape[1] - LANES
    for i in range(keep_ref.shape[0] // 8):
        rows, columns = slice(8 * i, 8 * i + 8), slice(i * half, (i + 1) * half)
        msg_ref[:, columns] = (keep_ref[rows, :half] + got_ref[rows, :half]).astype(BF16)
    pen = keep_ref[0:1, half : half + 1] + got_ref[0:1, half : half + 1]
    msg_ref[:, -LANES:] = spread3(pen, (8, LANES))


def sum_messages(refs):
    terms = [ref[...].astype(F32) for ref in refs]
    while len(terms) > 1:
        terms = [terms[i] + terms[i + 1] for i in range(0, len(terms), 2)]
    return terms[0]


def group_sum(*refs):
    total = sum_messages(refs[:-1])
    refs[-1][:, :-LANES] = total[:, :-LANES].astype(BF16)
    pen = jnp.sum(total[0:1, -LANES:], axis=1, keepdims=True)
    refs[-1][:, -LANES:] = spread3(pen, (8, LANES))


def pick_rows(device, rows, tokens):
    row = lax.broadcasted_iota(jnp.int32, (8, tokens), 0)
    column = lax.broadcasted_iota(jnp.int32, (8, tokens), 1)
    return jnp.where((column == device * rows + row) & (row < rows), 1.0, 0.0).astype(BF16)


def error_half(rows, target_ref, *refs):
    *msgs, out_ref, own_ref, pen_ref = refs
    tokens, half = target_ref.shape
    me = lax.axis_index("feat")
    total = sum_messages(msgs)
    recon = jnp.concatenate([total[:, i * half : (i + 1) * half] for i in range(tokens // 8)], axis=0)
    error = recon - target_ref[...].astype(F32)
    squares = jnp.sum(jnp.sum(error * error, axis=1, keepdims=True), axis=0, keepdims=True)
    narrow = recon.astype(BF16)
    own_ref[...] = jnp.dot(pick_rows(me, rows, tokens), narrow, preferred_element_type=F32)
    theirs = jnp.dot(pick_rows(me ^ 1, rows, tokens), narrow, preferred_element_type=F32)
    row = lax.broadcasted_iota(jnp.int32, (8, half), 0)
    parts = spread3(squares, (8, LANES)).astype(F32)
    parts = jnp.concatenate([parts, jnp.zeros((8, half - LANES), F32)], axis=1)
    out_ref[:tokens, :] = (error / ERROR_SCALE).astype(BF16)
    out_ref[tokens:, :] = jnp.where(row < rows, theirs, jnp.where(row == rows, parts, 0.0)).astype(BF16)
    pen = jnp.sum(total[0:1, -LANES:], axis=1, keepdims=True)
    pen_ref[...] = jnp.broadcast_to(pen, pen_ref.shape)


def act_grad(grad, dec):
    return lax.dot_general(dec, grad, NT, preferred_element_type=F32).T


def act_split(width):
    early = width // 2 // 256 * 256
    return early, width - early


def act_first(order, mine_ref, dec_ref, *outs):
    tokens, width = outs[0].shape[0], dec_ref.shape[2]
    early, late = act_split(width)
    side, me = lax.axis_index("feat") % 2, lax.axis_index("layer")
    span = pl.ds(pl.multiple_of(side * late, LANES), early)
    grad = jnp.where(side == 0, mine_ref[:tokens, :early], mine_ref[:tokens, width // 2 - early :])
    for k, out_ref in zip(order, outs):
        out_ref[...] = act_grad(grad, dec_ref[me ^ k, :, span])


def act_second(rows, order, mine_ref, got_ref, pen_ref, dec_ref, *refs):
    parts = refs[: len(order)]
    grad_ref, score_ref, *msgs = refs[len(order) :]
    tokens, half = grad_ref.shape[0], grad_ref.shape[1] // 2
    side, me = lax.axis_index("feat") % 2, lax.axis_index("layer")
    mine, got = mine_ref[:tokens, :], got_ref[:tokens, :]
    grad_ref[:, :half] = jnp.where(side == 0, mine, got)
    grad_ref[:, half:] = jnp.where(side == 0, got, mine)
    early, late = act_split(2 * half)
    span = pl.ds(pl.multiple_of((1 - side) * early, LANES), late)
    extra = got_ref[tokens:, :].astype(F32)
    mine_extra = mine_ref[tokens:, :].astype(F32)
    squares = jnp.sum(mine_extra[rows : rows + 1, :LANES], axis=1, keepdims=True)
    squares = squares + jnp.sum(extra[rows : rows + 1, :LANES], axis=1, keepdims=True)
    score = squares + 2.0 * ERROR_SCALE * PENALTY_WEIGHT * pen_ref[0:1, 0:1]
    score_ref[...] = jnp.broadcast_to(score, score_ref.shape)
    width = dec_ref.shape[1]
    for k, part_ref, msg in zip(order, parts, msgs):
        msg[:, :width] = (part_ref[...] + act_grad(grad_ref[:, span], dec_ref[me ^ k, :, span])).astype(BF16)
        msg[:, width:] = spread3(score, (tokens, LANES))


def write_decoder_grads(order, grad_ref, acts, out_hbm, buf, sems):
    me = lax.axis_index("layer")
    block = buf.shape[1]
    steps = acts[0].shape[1] // block
    copies = []
    for k, acts_ref in zip(order, acts):
        turned = acts_ref[...].T
        for i in range(steps):
            n = len(copies)
            span = slice(i * block, (i + 1) * block)
            buf[n] = jnp.dot(turned[span], grad_ref[...], preferred_element_type=F32).astype(BF16)
            copies.append(pltpu.make_async_copy(buf.at[n], out_hbm.at[me ^ k, pl.ds(i * block, block)], sems.at[n]))
            copies[-1].start()
    return copies


def first_grads(order, grad_ref, dec_ref, *refs):
    *acts, out_hbm, part_ref, buf, sems = refs
    copies = write_decoder_grads(order, grad_ref, acts, out_hbm, buf, sems)
    part_ref[...] = act_grad(grad_ref[...], dec_ref[lax.axis_index("layer")])
    for copy in copies:
        copy.wait()


def last_grads(count, order, grad_ref, own_ref, got_ref, x_ref, part_ref, gate_ref, sparse_ref, score_ref, *refs):
    *rest, _, dec_hbm, enc_hbm, loss_hbm, recon_hbm, dec_buf, dec_sems, enc_buf, enc_sems, loss_ref, loss_sem, recon_ref, recon_sem = refs
    acts, msgs = rest[: len(order)], rest[len(order) :]
    copies = []
    width = part_ref.shape[1]
    scores = [score_ref[0:1, 0:1]]
    for msg in msgs:
        scores.append(jnp.sum(msg[0:1, width:].astype(F32), axis=1, keepdims=True))
    while len(scores) > 1:
        scores = [scores[i] + scores[i + 1] for i in range(0, len(scores), 2)]
    loss_ref[...] = scores[0] / count
    copies.append(pltpu.make_async_copy(loss_ref, loss_hbm, loss_sem))
    copies[-1].start()
    total = part_ref[...]
    for msg in msgs:
        total = total + msg[:, :width].astype(F32)
    pre = jnp.where(gate_ref[...] > 0, total + sparse_ref[...], 0.0).astype(BF16)
    turned = x_ref[...].T
    block = enc_buf.shape[1]
    for i in range(enc_buf.shape[0]):
        span = slice(i * block, (i + 1) * block)
        enc_buf[i] = jnp.dot(turned[span], pre, preferred_element_type=F32).astype(BF16)
        copies.append(pltpu.make_async_copy(enc_buf.at[i], enc_hbm.at[pl.ds(i * block, block)], enc_sems.at[i]))
        copies[-1].start()
    copies += write_decoder_grads(order, grad_ref, acts, dec_hbm, dec_buf, dec_sems)
    tokens, half = grad_ref.shape[0], grad_ref.shape[1] // 2
    low = lax.axis_index("feat") % 2 == 0
    own, extra = own_ref[...], got_ref[tokens:, :].astype(F32)
    rows = recon_ref.shape[0]
    recon_ref[:, :half] = jnp.where(low, own, extra)[:rows].astype(BF16)
    recon_ref[:, half:] = jnp.where(low, extra, own)[:rows].astype(BF16)
    copies.append(pltpu.make_async_copy(recon_ref, recon_hbm, recon_sem))
    copies[-1].start()
    for copy in copies:
        copy.wait()


def body(residual_in, enc_weight, thresholds, dec_weight, target):
    layers, feats = lax.axis_size("layer"), lax.axis_size("feat")
    rows, width = residual_in.shape[1:]
    features = enc_weight.shape[2]
    tokens, half = rows * feats, width // 2
    sources = dec_weight.shape[0]
    decoder = dec_weight[:, 0]

    height = -(-2 * rows // 8) * 8
    mine = (residual_in[0], target[0])
    *own, cutoff = call(
        load_own,
        [shape((rows, width), BF16)] * 2 + [shape((1, features), F32)],
        [in_hbm(part) for part in (*mine, thresholds)],
        "load_own",
        scratch=[pltpu.VMEM((1, features), jnp.int32), pltpu.SemaphoreType.DMA((3,))],
        in_specs=[ANY] * 3,
        bytes_accessed=2 * width * features,
    )
    got = [swap(part, "feat", 1) for part in mine]
    (block,) = call(pack, [shape((height, width + half), BF16)], (*own, *got), "pack")
    (encoder,) = call(
        fetch,
        [shape((width, features), BF16)],
        (block, in_hbm(enc_weight[0])),
        "fetch",
        scratch=[pltpu.SemaphoreType.DMA(())],
        in_specs=[ANY] * 2,
        bytes_accessed=4 * width * features,
    )
    blocks, bit = [block], 2
    while bit < feats:
        pair = (bit, 2 * bit, 3 * bit) if 2 * bit < feats else (bit,)
        blocks = [block] + [swap(block, "feat", k) for k in pair]
        bit <<= len(pair) // 2 + 1
        if bit < feats:
            (block,) = call(stack, [shape((bit // 2 * height, width + half), BF16)], blocks, "stack")
    x, targets, acts, gate = call(
        functools.partial(encode, rows, height),
        [shape((tokens, width), BF16), shape((tokens, half), BF16)]
        + [shape((tokens, features), BF16), shape((tokens, features), F32)],
        (*blocks, encoder, cutoff),
        "encode",
        flops=2 * tokens * width * features,
        bytes_accessed=2 * width * features,
    )
    back = exchange_order(layers)
    order = back[::-1]
    others = [swap(acts, "layer", k) for k in order]
    pieces = max(1, features // 256)
    total, sparse, pen = call(
        recon_own,
        [shape((tokens, width), F32), shape((tokens, features), F32), shape((8, LANES), F32)],
        (acts, in_hbm(decoder)),
        "recon_own",
        scratch=[pltpu.VMEM((pieces, features // pieces, width), BF16), pltpu.SemaphoreType.DMA((pieces,))],
        in_specs=[WHOLE, ANY],
        limit=12,
        flops=2 * tokens * width * features,
        bytes_accessed=2 * width * features,
    )
    send, keep = (
        call(
            functools.partial(recon_half, theirs, order),
            [shape((tokens, half + LANES), F32)],
            (total, pen, decoder, *others),
            name,
            flops=tokens * width * features * (sources - 1),
            bytes_accessed=(sources - 1) * width * features,
        )[0]
        for theirs, name in ((1, "recon_send"), (0, "recon_keep"))
    )
    (msg,) = call(pair_sum, [shape((8, tokens // 8 * half + LANES), BF16)], (keep, swap(send, "feat", 1)), "pair_sum")
    bit = 2
    while bit < feats:
        pair = (bit, 2 * bit, 3 * bit) if 2 * bit < feats else (bit,)
        msgs = [msg] + [swap(msg, "feat", k) for k in pair]
        bit <<= len(pair) // 2 + 1
        if bit < feats:
            (msg,) = call(group_sum, [shape(msg.shape, BF16)], msgs, "group_sum")
    mine, own_rows, pen_all = call(
        functools.partial(error_half, rows),
        [shape((tokens + 8, half), BF16), shape((8, half), F32), shape((8, LANES), F32)],
        (targets, *msgs),
        "error_half",
    )
    parts = call(
        functools.partial(act_first, back),
        [shape((tokens, features), F32)] * (layers - 1),
        (mine, decoder),
        "act_first",
        flops=tokens * width * features * (sources - 1),
        bytes_accessed=(sources - 1) * width * features,
    )
    theirs = swap(mine, "feat", 1)
    grad, score, *sends = call(
        functools.partial(act_second, rows, back),
        [shape((tokens, width), BF16), shape((8, LANES), F32)] + [shape((tokens, features + LANES), BF16)] * (layers - 1),
        (mine, theirs, pen_all, decoder, *parts),
        "act_second",
        flops=tokens * width * features * (sources - 1),
        bytes_accessed=(sources - 1) * width * features,
    )
    gots = [swap(send, "layer", k) for send, k in zip(sends, back)]
    first, steps, block = sources - 1, max(1, features // 128), 128
    last = sources - first
    dec_grad, part = call(
        functools.partial(first_grads, (0, *order[: first - 1])),
        [shape((sources, features, width), BF16), shape((tokens, features), F32)],
        (grad, decoder, acts, *others[: first - 1]),
        "first_grads",
        scratch=[pltpu.VMEM((first * steps, features // steps, width), BF16), pltpu.SemaphoreType.DMA((first * steps,))],
        limit=24,
        out_specs=[ANY, WHOLE],
        flops=2 * tokens * width * features * (first + 1),
        bytes_accessed=2 * first * width * features,
    )
    args = (grad, own_rows, theirs, x, part, gate, sparse, score, *others[first - 1 :], *gots, dec_grad)
    dec_grad, enc_grad, loss, recon = call(
        functools.partial(last_grads, layers * tokens * width, order[first - 1 :]),
        [shape((sources, features, width), BF16), shape((width, features), BF16), shape((1, 1), F32), shape((rows, width), BF16)],
        args,
        "last_grads",
        scratch=[
            pltpu.VMEM((last * steps, features // steps, width), BF16),
            pltpu.SemaphoreType.DMA((last * steps,)),
            pltpu.VMEM((width // block, block, features), BF16),
            pltpu.SemaphoreType.DMA((width // block,)),
            pltpu.VMEM((1, 1), F32),
            pltpu.SemaphoreType.DMA(()),
            pltpu.VMEM((rows, width), BF16),
            pltpu.SemaphoreType.DMA(()),
        ],
        in_specs=[WHOLE] * (len(args) - 1) + [ANY],
        out_specs=[ANY] * 4,
        limit=24,
        aliases={len(args) - 1: 0},
        flops=2 * tokens * width * features * (last + 1),
        bytes_accessed=2 * (last + 1) * width * features,
    )
    return loss[0, 0], recon[None], dec_grad[:, None], enc_grad[None]


def solution(mesh):
    return jax.shard_map(
        body,
        mesh=mesh,
        in_specs=(
            P("layer", "feat", None),
            P("layer", None, "feat"),
            P("layer", "feat"),
            P(None, "layer", "feat", None),
            P("layer", "feat", None),
        ),
        out_specs=(
            P(),
            P("layer", "feat", None),
            P(None, "layer", "feat", None),
            P("layer", None, "feat"),
        ),
        check_vma=False,
    )
```

```python
import functools

import jax
import jax.numpy as jnp
from jax import lax
from jax.experimental import pallas as pl
from jax.experimental.pallas import tpu as pltpu
from jax.sharding import PartitionSpec as P

ERROR_SCALE = 32.0
PENALTY_WEIGHT = 4.0
F32 = jnp.float32
BF16 = jnp.bfloat16
LANES = 128
MIB = 1 << 20
WHOLE = pl.BlockSpec(memory_space=pltpu.VMEM)
ANY = pl.BlockSpec(memory_space=pl.ANY)
NT = (((1,), (1,)), ((), ()))
TN = (((0,), (0,)), ((), ()))


def in_hbm(x):
    return pltpu.with_memory_space_constraint(x, pltpu.HBM)


def shape(dims, dtype):
    return jax.ShapeDtypeStruct(dims, dtype)


def call(body, outs, args, name, scratch=(), limit=16, in_specs=None, out_specs=None, aliases=None, flops=0, bytes_accessed=0):
    return pl.pallas_call(
        body,
        out_shape=outs,
        in_specs=in_specs or [WHOLE] * len(args),
        out_specs=out_specs or [WHOLE] * len(outs),
        scratch_shapes=list(scratch),
        input_output_aliases=aliases or {},
        compiler_params=pltpu.CompilerParams(vmem_limit_bytes=limit * MIB),
        cost_estimate=pl.CostEstimate(flops=flops, bytes_accessed=bytes_accessed, transcendentals=0),
        name=name,
    )(*args)


def swap(x, axis, bits):
    size = lax.axis_size(axis)
    return lax.ppermute(x, axis, [(i, i ^ bits) for i in range(size)])


def exchange_order(size):
    return (2, 3, 1) if size == 4 else tuple(range(1, size))


def split3(value):
    high = value.astype(BF16)
    rest = value - high.astype(F32)
    middle = rest.astype(BF16)
    low = (rest - middle.astype(F32)).astype(BF16)
    return high, middle, low


def spread3(value, dims):
    high, middle, low = (part.astype(F32) for part in split3(value))
    lane = lax.broadcasted_iota(jnp.int32, dims, 1)
    block = jnp.where(lane == 0, high, jnp.where(lane == 1, middle, jnp.where(lane == 2, low, 0.0)))
    return block.astype(BF16)


def load_own(res_hbm, target_hbm, thr_hbm, res_ref, target_ref, cutoff_ref, thr_ref, sems):
    places = ((res_hbm, res_ref), (target_hbm, target_ref), (thr_hbm, thr_ref))
    copies = [pltpu.make_async_copy(*place, sems.at[i]) for i, place in enumerate(places)]
    for copy in copies:
        copy.start()
    for copy in copies:
        copy.wait()
    cutoff_ref[...] = (thr_ref[...].astype(F32) + 0.5) / 2048.0


def pack(res_ref, target_ref, res_got_ref, target_got_ref, out_ref):
    rows, width = res_ref.shape
    half = width // 2
    low = lax.axis_index("feat") % 2 == 0
    out_ref[...] = jnp.zeros_like(out_ref)
    for start, res, target in ((0, res_ref, target_ref), (rows, res_got_ref, target_got_ref)):
        out_ref[start : start + rows, :width] = res[...]
        out_ref[start : start + rows, width:] = jnp.where(low, target[:, :half], target[:, half:])


def stack(*refs):
    out_ref = refs[-1]
    height = refs[0].shape[0]
    for i, ref in enumerate(refs[:-1]):
        out_ref[i * height : (i + 1) * height] = ref[...]


def fetch(_, src_hbm, out_ref, sem):
    copy = pltpu.make_async_copy(src_hbm, out_ref, sem)
    copy.start()
    copy.wait()


def gather_rows(rows, height, tokens, blocks):
    dims = (tokens, blocks.shape[0])
    token = lax.broadcasted_iota(jnp.int32, dims, 0)
    place = lax.broadcasted_iota(jnp.int32, dims, 1)
    inner = place % height
    second = (inner >= rows).astype(jnp.int32)
    device = (place // height * 2 + second) ^ lax.axis_index("feat")
    chosen = (inner < 2 * rows) & (device * rows + inner - second * rows == token)
    picked = jnp.dot(jnp.where(chosen, 1.0, 0.0).astype(BF16), blocks, preferred_element_type=F32)
    return picked.astype(BF16)


def encode(rows, height, *refs):
    *block_refs, enc_ref, cutoff_ref, x_ref, target_ref, acts_ref, gate_ref, sparse_ref, pen_ref = refs
    tokens = x_ref.shape[0]
    blocks = jnp.concatenate([ref[...] for ref in block_refs], axis=0)
    gathered = gather_rows(rows, height, tokens, blocks)
    x = gathered[:, : x_ref.shape[1]]
    x_ref[...] = x
    target_ref[...] = gathered[:, x_ref.shape[1] :]
    preact = jnp.dot(x, enc_ref[...], preferred_element_type=F32)
    firing = preact > cutoff_ref[...]
    acts = jnp.where(firing, preact, 0.0).astype(BF16)
    acts_ref[...] = acts
    wide = acts.astype(F32)
    magnitude = jnp.sum(jnp.abs(wide), axis=0, keepdims=True) / tokens
    sign = jnp.where(wide > 0, 1.0, jnp.where(wide < 0, -1.0, 0.0))
    gate_ref[...] = firing.astype(F32)
    sparse_ref[...] = 2.0 * PENALTY_WEIGHT * magnitude * sign / tokens
    pen = jnp.sum(magnitude * magnitude, axis=1, keepdims=True)
    pen_ref[...] = jnp.broadcast_to(pen, pen_ref.shape)


def recon_own(acts_ref, dec_hbm, total_ref, buf, sems):
    me = lax.axis_index("layer")
    pieces = buf.shape[0]
    block = buf.shape[1]
    copies = []
    for i in range(pieces):
        copies.append(pltpu.make_async_copy(dec_hbm.at[me, pl.ds(i * block, block)], buf.at[i], sems.at[i]))
        copies[-1].start()
    total = jnp.zeros(total_ref.shape, F32)
    for i in range(pieces):
        copies[i].wait()
        total = total + jnp.dot(acts_ref[:, i * block : (i + 1) * block], buf[i], preferred_element_type=F32)
    total_ref[...] = total


def recon_half(theirs, order, total_ref, pen_ref, dec_ref, *refs):
    *acts, out_ref = refs
    me = lax.axis_index("layer")
    half = dec_ref.shape[2] // 2
    span = pl.ds(pl.multiple_of((lax.axis_index("feat") + theirs) % 2 * half, half), half)
    total = total_ref[:, span]
    for k, acts_ref in zip(order, acts):
        total = total + jnp.dot(acts_ref[...], dec_ref[me ^ k, :, span], preferred_element_type=F32)
    out_ref[:, :half] = total
    out_ref[:, half:] = jnp.broadcast_to(pen_ref[0:1, :], (total.shape[0], LANES))


def pair_sum(keep_ref, got_ref, msg_ref):
    half = keep_ref.shape[1] - LANES
    for i in range(keep_ref.shape[0] // 8):
        rows, columns = slice(8 * i, 8 * i + 8), slice(i * half, (i + 1) * half)
        msg_ref[:, columns] = (keep_ref[rows, :half] + got_ref[rows, :half]).astype(BF16)
    pen = keep_ref[0:1, half : half + 1] + got_ref[0:1, half : half + 1]
    msg_ref[:, -LANES:] = spread3(pen, (8, LANES))


def sum_messages(refs):
    terms = [ref[...].astype(F32) for ref in refs]
    while len(terms) > 1:
        terms = [terms[i] + terms[i + 1] for i in range(0, len(terms), 2)]
    return terms[0]


def group_sum(*refs):
    total = sum_messages(refs[:-1])
    refs[-1][:, :-LANES] = total[:, :-LANES].astype(BF16)
    pen = jnp.sum(total[0:1, -LANES:], axis=1, keepdims=True)
    refs[-1][:, -LANES:] = spread3(pen, (8, LANES))


def pick_rows(device, rows, tokens):
    row = lax.broadcasted_iota(jnp.int32, (8, tokens), 0)
    column = lax.broadcasted_iota(jnp.int32, (8, tokens), 1)
    return jnp.where((column == device * rows + row) & (row < rows), 1.0, 0.0).astype(BF16)


def error_half(rows, target_ref, *refs):
    *msgs, out_ref, own_ref, pen_ref = refs
    tokens, half = target_ref.shape
    me = lax.axis_index("feat")
    total = sum_messages(msgs)
    recon = jnp.concatenate([total[:, i * half : (i + 1) * half] for i in range(tokens // 8)], axis=0)
    error = recon - target_ref[...].astype(F32)
    squares = jnp.sum(jnp.sum(error * error, axis=1, keepdims=True), axis=0, keepdims=True)
    narrow = recon.astype(BF16)
    own_ref[...] = jnp.dot(pick_rows(me, rows, tokens), narrow, preferred_element_type=F32)
    theirs = jnp.dot(pick_rows(me ^ 1, rows, tokens), narrow, preferred_element_type=F32)
    row = lax.broadcasted_iota(jnp.int32, (8, half), 0)
    parts = spread3(squares, (8, LANES)).astype(F32)
    parts = jnp.concatenate([parts, jnp.zeros((8, half - LANES), F32)], axis=1)
    out_ref[:tokens, :] = (error / ERROR_SCALE).astype(BF16)
    out_ref[tokens:, :] = jnp.where(row < rows, theirs, jnp.where(row == rows, parts, 0.0)).astype(BF16)
    pen = jnp.sum(total[0:1, -LANES:], axis=1, keepdims=True)
    pen_ref[...] = jnp.broadcast_to(pen, pen_ref.shape)


def act_grad(grad, dec):
    return lax.dot_general(dec, grad, NT, preferred_element_type=F32).T


def act_split(width):
    early = width // 2 // 256 * 256
    return early, width - early


def act_first(order, mine_ref, dec_ref, *outs):
    tokens, width = outs[0].shape[0], dec_ref.shape[2]
    early, late = act_split(width)
    side, me = lax.axis_index("feat") % 2, lax.axis_index("layer")
    span = pl.ds(pl.multiple_of(side * late, LANES), early)
    grad = jnp.where(side == 0, mine_ref[:tokens, :early], mine_ref[:tokens, width // 2 - early :])
    for k, out_ref in zip(order, outs):
        out_ref[...] = act_grad(grad, dec_ref[me ^ k, :, span])


def act_second(rows, order, mine_ref, got_ref, pen_ref, dec_ref, *refs):
    parts = refs[: len(order)]
    grad_ref, score_ref, *msgs = refs[len(order) :]
    tokens, half = grad_ref.shape[0], grad_ref.shape[1] // 2
    side, me = lax.axis_index("feat") % 2, lax.axis_index("layer")
    mine, got = mine_ref[:tokens, :], got_ref[:tokens, :]
    grad_ref[:, :half] = jnp.where(side == 0, mine, got)
    grad_ref[:, half:] = jnp.where(side == 0, got, mine)
    early, late = act_split(2 * half)
    span = pl.ds(pl.multiple_of((1 - side) * early, LANES), late)
    extra = got_ref[tokens:, :].astype(F32)
    mine_extra = mine_ref[tokens:, :].astype(F32)
    squares = jnp.sum(mine_extra[rows : rows + 1, :LANES], axis=1, keepdims=True)
    squares = squares + jnp.sum(extra[rows : rows + 1, :LANES], axis=1, keepdims=True)
    score = squares + 2.0 * ERROR_SCALE * PENALTY_WEIGHT * pen_ref[0:1, 0:1]
    score_ref[...] = jnp.broadcast_to(score, score_ref.shape)
    width = dec_ref.shape[1]
    for k, part_ref, msg in zip(order, parts, msgs):
        msg[:, :width] = (part_ref[...] + act_grad(grad_ref[:, span], dec_ref[me ^ k, :, span])).astype(BF16)
        msg[:, width:] = spread3(score, (tokens, LANES))


def write_decoder_grads(order, grad_ref, acts, out_hbm, buf, sems):
    me = lax.axis_index("layer")
    block = buf.shape[1]
    steps = acts[0].shape[1] // block
    copies = []
    for k, acts_ref in zip(order, acts):
        turned = acts_ref[...].T
        for i in range(steps):
            n = len(copies)
            span = slice(i * block, (i + 1) * block)
            buf[n] = jnp.dot(turned[span], grad_ref[...], preferred_element_type=F32).astype(BF16)
            copies.append(pltpu.make_async_copy(buf.at[n], out_hbm.at[me ^ k, pl.ds(i * block, block)], sems.at[n]))
            copies[-1].start()
    return copies


def first_grads(order, grad_ref, dec_ref, *refs):
    *acts, out_hbm, part_ref, buf, sems = refs
    copies = write_decoder_grads(order, grad_ref, acts, out_hbm, buf, sems)
    part_ref[...] = act_grad(grad_ref[...], dec_ref[lax.axis_index("layer")])
    for copy in copies:
        copy.wait()


def last_grads(count, order, grad_ref, own_ref, got_ref, x_ref, part_ref, gate_ref, sparse_ref, score_ref, *refs):
    *rest, _, dec_hbm, enc_hbm, loss_hbm, recon_hbm, dec_buf, dec_sems, enc_buf, enc_sems, loss_ref, loss_sem, recon_ref, recon_sem = refs
    acts, msgs = rest[: len(order)], rest[len(order) :]
    copies = []
    width = part_ref.shape[1]
    scores = [score_ref[0:1, 0:1]]
    for msg in msgs:
        scores.append(jnp.sum(msg[0:1, width:].astype(F32), axis=1, keepdims=True))
    while len(scores) > 1:
        scores = [scores[i] + scores[i + 1] for i in range(0, len(scores), 2)]
    loss_ref[...] = scores[0] / count
    copies.append(pltpu.make_async_copy(loss_ref, loss_hbm, loss_sem))
    copies[-1].start()
    total = part_ref[...]
    for msg in msgs:
        total = total + msg[:, :width].astype(F32)
    pre = jnp.where(gate_ref[...] > 0, total + sparse_ref[...], 0.0).astype(BF16)
    turned = x_ref[...].T
    block = enc_buf.shape[1]
    for i in range(enc_buf.shape[0]):
        span = slice(i * block, (i + 1) * block)
        enc_buf[i] = jnp.dot(turned[span], pre, preferred_element_type=F32).astype(BF16)
        copies.append(pltpu.make_async_copy(enc_buf.at[i], enc_hbm.at[pl.ds(i * block, block)], enc_sems.at[i]))
        copies[-1].start()
    copies += write_decoder_grads(order, grad_ref, acts, dec_hbm, dec_buf, dec_sems)
    tokens, half = grad_ref.shape[0], grad_ref.shape[1] // 2
    low = lax.axis_index("feat") % 2 == 0
    own, extra = own_ref[...], got_ref[tokens:, :].astype(F32)
    rows = recon_ref.shape[0]
    recon_ref[:, :half] = jnp.where(low, own, extra)[:rows].astype(BF16)
    recon_ref[:, half:] = jnp.where(low, extra, own)[:rows].astype(BF16)
    copies.append(pltpu.make_async_copy(recon_ref, recon_hbm, recon_sem))
    copies[-1].start()
    for copy in copies:
        copy.wait()


def body(residual_in, enc_weight, thresholds, dec_weight, target):
    layers, feats = lax.axis_size("layer"), lax.axis_size("feat")
    rows, width = residual_in.shape[1:]
    features = enc_weight.shape[2]
    tokens, half = rows * feats, width // 2
    sources = dec_weight.shape[0]
    decoder = dec_weight[:, 0]

    height = -(-2 * rows // 8) * 8
    mine = (residual_in[0], target[0])
    *own, cutoff = call(
        load_own,
        [shape((rows, width), BF16)] * 2 + [shape((1, features), F32)],
        [in_hbm(part) for part in (*mine, thresholds)],
        "load_own",
        scratch=[pltpu.VMEM((1, features), jnp.int32), pltpu.SemaphoreType.DMA((3,))],
        in_specs=[ANY] * 3,
        bytes_accessed=2 * width * features,
    )
    got = [swap(part, "feat", 1) for part in mine]
    (block,) = call(pack, [shape((height, width + half), BF16)], (*own, *got), "pack")
    (encoder,) = call(
        fetch,
        [shape((width, features), BF16)],
        (block, in_hbm(enc_weight[0])),
        "fetch",
        scratch=[pltpu.SemaphoreType.DMA(())],
        in_specs=[ANY] * 2,
        bytes_accessed=4 * width * features,
    )
    blocks, bit = [block], 2
    while bit < feats:
        pair = (bit, 2 * bit, 3 * bit) if 2 * bit < feats else (bit,)
        blocks = [block] + [swap(block, "feat", k) for k in pair]
        bit <<= len(pair) // 2 + 1
        if bit < feats:
            (block,) = call(stack, [shape((bit // 2 * height, width + half), BF16)], blocks, "stack")
    x, targets, acts, gate, sparse, pen = call(
        functools.partial(encode, rows, height),
        [shape((tokens, width), BF16), shape((tokens, half), BF16)]
        + [shape((tokens, features), BF16), shape((tokens, features), F32), shape((tokens, features), F32), shape((8, LANES), F32)],
        (*blocks, encoder, cutoff),
        "encode",
        flops=2 * tokens * width * features,
        bytes_accessed=2 * width * features,
    )
    back = exchange_order(layers)
    order = back[::-1]
    others = [swap(acts, "layer", k) for k in order]
    pieces = max(1, features // 512)
    (total,) = call(
        recon_own,
        [shape((tokens, width), F32)],
        (acts, in_hbm(decoder)),
        "recon_own",
        scratch=[pltpu.VMEM((pieces, features // pieces, width), BF16), pltpu.SemaphoreType.DMA((pieces,))],
        in_specs=[WHOLE, ANY],
        limit=12,
        flops=2 * tokens * width * features,
        bytes_accessed=2 * width * features,
    )
    send, keep = (
        call(
            functools.partial(recon_half, theirs, order),
            [shape((tokens, half + LANES), F32)],
            (total, pen, decoder, *others),
            name,
            flops=tokens * width * features * (sources - 1),
            bytes_accessed=(sources - 1) * width * features,
        )[0]
        for theirs, name in ((1, "recon_send"), (0, "recon_keep"))
    )
    (msg,) = call(pair_sum, [shape((8, tokens // 8 * half + LANES), BF16)], (keep, swap(send, "feat", 1)), "pair_sum")
    bit = 2
    while bit < feats:
        pair = (bit, 2 * bit, 3 * bit) if 2 * bit < feats else (bit,)
        msgs = [msg] + [swap(msg, "feat", k) for k in pair]
        bit <<= len(pair) // 2 + 1
        if bit < feats:
            (msg,) = call(group_sum, [shape(msg.shape, BF16)], msgs, "group_sum")
    mine, own_rows, pen_all = call(
        functools.partial(error_half, rows),
        [shape((tokens + 8, half), BF16), shape((8, half), F32), shape((8, LANES), F32)],
        (targets, *msgs),
        "error_half",
    )
    parts = call(
        functools.partial(act_first, back),
        [shape((tokens, features), F32)] * (layers - 1),
        (mine, decoder),
        "act_first",
        flops=tokens * width * features * (sources - 1),
        bytes_accessed=(sources - 1) * width * features,
    )
    theirs = swap(mine, "feat", 1)
    grad, score, *sends = call(
        functools.partial(act_second, rows, back),
        [shape((tokens, width), BF16), shape((8, LANES), F32)] + [shape((tokens, features + LANES), BF16)] * (layers - 1),
        (mine, theirs, pen_all, decoder, *parts),
        "act_second",
        flops=tokens * width * features * (sources - 1),
        bytes_accessed=(sources - 1) * width * features,
    )
    gots = [swap(send, "layer", k) for send, k in zip(sends, back)]
    first, steps, block = sources - 1, max(1, features // 128), 128
    last = sources - first
    dec_grad, part = call(
        functools.partial(first_grads, (0, *order[: first - 1])),
        [shape((sources, features, width), BF16), shape((tokens, features), F32)],
        (grad, decoder, acts, *others[: first - 1]),
        "first_grads",
        scratch=[pltpu.VMEM((first * steps, features // steps, width), BF16), pltpu.SemaphoreType.DMA((first * steps,))],
        limit=24,
        out_specs=[ANY, WHOLE],
        flops=2 * tokens * width * features * (first + 1),
        bytes_accessed=2 * first * width * features,
    )
    args = (grad, own_rows, theirs, x, part, gate, sparse, score, *others[first - 1 :], *gots, dec_grad)
    dec_grad, enc_grad, loss, recon = call(
        functools.partial(last_grads, layers * tokens * width, order[first - 1 :]),
        [shape((sources, features, width), BF16), shape((width, features), BF16), shape((1, 1), F32), shape((rows, width), BF16)],
        args,
        "last_grads",
        scratch=[
            pltpu.VMEM((last * steps, features // steps, width), BF16),
            pltpu.SemaphoreType.DMA((last * steps,)),
            pltpu.VMEM((width // block, block, features), BF16),
            pltpu.SemaphoreType.DMA((width // block,)),
            pltpu.VMEM((1, 1), F32),
            pltpu.SemaphoreType.DMA(()),
            pltpu.VMEM((rows, width), BF16),
            pltpu.SemaphoreType.DMA(()),
        ],
        in_specs=[WHOLE] * (len(args) - 1) + [ANY],
        out_specs=[ANY] * 4,
        limit=24,
        aliases={len(args) - 1: 0},
        flops=2 * tokens * width * features * (last + 1),
        bytes_accessed=2 * (last + 1) * width * features,
    )
    return loss[0, 0], recon[None], dec_grad[:, None], enc_grad[None]


def solution(mesh):
    return jax.shard_map(
        body,
        mesh=mesh,
        in_specs=(
            P("layer", "feat", None),
            P("layer", None, "feat"),
            P("layer", "feat"),
            P(None, "layer", "feat", None),
            P("layer", "feat", None),
        ),
        out_specs=(
            P(),
            P("layer", "feat", None),
            P(None, "layer", "feat", None),
            P("layer", None, "feat"),
        ),
        check_vma=False,
    )
```
